128 devices in a mesh: dp: 8 (over z_lo, x), vocab: 16 (over z_hi, y, core).
Axes of the slice: x: 4, y: 4, z: 4 (z_hi: 2, z_lo: 2; z = z_hi * 2 + z_lo), core: 2. Of those that a mesh axis runs over, the one named last changes fastest.
Arguments:
- hidden: bfloat16 [2, 8, 256, 4096], P(None, 'dp'), may hold values from -6 to 6
- weight: bfloat16 [32000, 4096], P('vocab'), may hold values from -0.09375 to 0.09375
- bias: float32 [32000], P('vocab'), may hold values from -1 to 0
- positions: int32 [2, 8, 32000], P(None, 'dp', 'vocab'), may hold values from 0 to 255
- lengths: int32 [2, 8], P(None, 'dp'), may hold values from 64 to 256
- pairs: int32 [8, 2], P('dp'), may hold values from 0 to 7
- margins: float32 [8], P('dp'), may hold values from -4 to 4
Outputs:
- grad_hidden: bfloat16 [2, 8, 256, 4096], P(None, 'dp', 'vocab')
- grad_weight: float32 [32000, 4096], P('vocab', 'dp')
The draws below stay inside these ranges and needn't reach their ends.
Inputs may be any that keep to these rules, and one draw needn't show every extreme that they name: positions of tokens within a sequence, padded ones included. `pairs`: indices of passages in the whole batch; a pair's two may coincide.
All inputs are finite; a program needn't handle non-finite values.
Results may differ from the reference program's by a relative error of at most 0.02.
Values may be sent and summed in bfloat16 or wider, within the bound.
A program may use at most 128 MiB of HBM per device.

```python
import jax
import jax.numpy as jnp
from jax import lax

D = 4096
V = 32000
L = 256
BDEV = 1
GROUP_COUNT = 8
N_DP = 8


def with_ends(values, rng, smallest, top_value):
    place = [jax.random.randint(jax.random.fold_in(rng, axis), (), 0, length) for axis, length in enumerate(values.shape)]
    longest = values.shape.index(max(values.shape))
    neighbour = place[:longest] + [(place[longest] + 1) % values.shape[longest]] + place[longest + 1:]
    return values.at[tuple(place)].set(smallest).at[tuple(neighbour)].set(top_value)


def block_scale(own_key, dims, pieces, smallest, high):
    factor_of, own = 1.0, jax.random.fold_in(own_key, 6)
    for position, blocks in pieces:
        draws = jnp.exp(jax.random.uniform(jax.random.fold_in(own, position), (blocks,), jnp.float32, smallest / len(pieces), high / len(pieces)))
        factor_of = factor_of * jnp.repeat(draws, dims[position] // blocks).reshape([-1 if axis == position else 1 for axis in range(len(dims))])
    return factor_of


def scatter_about(rng, shape, deviation, most, shards=(), kind=jnp.bfloat16):
    result = jax.random.normal(rng, shape, jnp.float32) * deviation
    if len(shards) > 0:
        result = block_scale(rng, shape, shards, -0.22, 0.18) * result
    return jnp.clip(result, min=-most, max=most).astype(kind)


def setup_inputs(seed: int = 0) -> dict:
    arg_keys = jax.random.split(jax.random.key(seed), 8)
    return {
        "hidden": scatter_about(arg_keys[0], (2, GROUP_COUNT, L, D), 1.0, 6.0, ((1, 8),)),
        "weight": scatter_about(arg_keys[1], (V, D), D ** -0.5, 0.09375, ((0, 16),)),
        "bias": jnp.clip(-1.0 + 1.0 * jax.random.uniform(arg_keys[2], (V,), jnp.float32) ** block_scale(arg_keys[2], (V,), ((0, 16),), -0.2, 0.2), -1.0, 0.0),
        "positions": with_ends(jax.random.randint(arg_keys[3], (2, GROUP_COUNT, V), 0, L), jax.random.fold_in(arg_keys[3], 1), 0, L - 1).astype(jnp.int32),
        "lengths": with_ends(jax.random.randint(arg_keys[4], (2, GROUP_COUNT), L // 4, L + 1), jax.random.fold_in(arg_keys[4], 1), L // 4, L).astype(jnp.int32),
        "pairs": with_ends(jax.random.randint(arg_keys[5], (GROUP_COUNT, 2), 0, GROUP_COUNT), jax.random.fold_in(arg_keys[5], 1), 0, GROUP_COUNT - 1).astype(jnp.int32),
        "margins": scatter_about(arg_keys[6], (GROUP_COUNT,), 1.0, 4.0, ((0, 8),), jnp.float32),
    }


logit_divisor = 16.0
objective_factor = 256.0
regularizer_coefficient = 0.1


def reference(hidden, weight, bias, positions, lengths, pairs, margins):
    flat_hidden = hidden.reshape(2 * GROUP_COUNT, L, D)
    flat_pos = positions.reshape(2 * GROUP_COUNT, V)

    def select_one(args):
        states, spots = args
        logits = jnp.dot(states, weight.T, preferred_element_type=jnp.float32) + bias
        return jnp.take_along_axis(logits, spots[None, :], axis=0)[0]

    selected = lax.map(select_one, (flat_hidden, flat_pos)).reshape(2, GROUP_COUNT, V)
    valid = positions < lengths[:, :, None]
    pooled = jnp.where(valid, jnp.log1p(jnp.maximum(selected, 0.0)), 0.0)
    request_vectors = pooled[0]
    document_vectors = pooled[1]
    relevance_logits = jnp.dot(request_vectors, document_vectors.T, precision=lax.Precision.HIGHEST) / logit_divisor
    columns = lax.broadcasted_iota(jnp.int32, (GROUP_COUNT, GROUP_COUNT), 1)
    sign = (columns == pairs[:, 0:1]).astype(jnp.float32) - (columns == pairs[:, 1:2]).astype(jnp.float32)
    delta = jnp.sum(relevance_logits * sign, axis=1)
    request_average = jnp.sum(request_vectors, axis=0) / GROUP_COUNT
    document_average = jnp.sum(document_vectors, axis=0) / GROUP_COUNT
    relevance_derivative = (objective_factor * 2.0 * (delta - margins) / GROUP_COUNT)[:, None] * sign
    request_derivative = jnp.dot(relevance_derivative, document_vectors, precision=lax.Precision.HIGHEST) / logit_divisor + objective_factor * regularizer_coefficient * 2.0 * request_average / GROUP_COUNT
    document_derivative = jnp.dot(relevance_derivative.T, request_vectors, precision=lax.Precision.HIGHEST) / logit_divisor + objective_factor * regularizer_coefficient * 2.0 * document_average / GROUP_COUNT
    drep = jnp.stack([request_derivative, document_derivative])
    dsel = jnp.where((selected > 0.0) & valid, drep / (1.0 + jnp.maximum(selected, 0.0)), 0.0)
    token_index = lax.broadcasted_iota(jnp.int32, (2, BDEV, L, V), 2)
    grad_parts = []
    total = jnp.zeros((V, D), jnp.float32)
    for group in range(N_DP):
        lo = group * BDEV
        spots = positions[:, lo:lo + BDEV]
        grads = jnp.where(token_index == spots[:, :, None, :], dsel[:, lo:lo + BDEV, None, :], 0.0).astype(jnp.bfloat16)
        grads = grads.reshape(2 * BDEV * L, V)
        states = hidden[:, lo:lo + BDEV].reshape(2 * BDEV * L, D)
        part_hidden = jnp.dot(grads, weight, preferred_element_type=jnp.float32).astype(jnp.bfloat16)
        grad_parts.append(part_hidden.reshape(2, BDEV, L, D))
        partway_result = jnp.dot(grads.T, states, preferred_element_type=jnp.float32).astype(jnp.bfloat16)
        partway_result = lax.optimization_barrier(partway_result)
        total = total + partway_result.astype(jnp.float32)
    grad_hidden = jnp.concatenate(grad_parts, axis=1)
    return grad_hidden, total
```

```python
import jax
import jax.numpy as jnp
from jax import lax
from jax.experimental import pallas as pl
from jax.experimental.pallas import tpu as pltpu
from jax.sharding import PartitionSpec as P

logit_divisor = 16.0
objective_factor = 256.0
regularizer_coefficient = 0.1

BF = jnp.bfloat16
F32 = jnp.float32
MESH = pl.DeviceIdType.MESH

V = 2000
VP = 2048
D = 4096
L = 256
NK = 8
NJ = 16
DB = 512
FC = 512
NF = VP // FC
HC = 512
NH = D // HC
HA = HC // 2
WC = 512
NW = VP // WC


def kernel(
    h_hbm,
    w_hbm,
    bias,
    pos_in,
    lens,
    pairs,
    margins,
    gh_out,
    gw_out,
    wv,
    hv,
    hx,
    g,
    gc,
    gwst,
    sibs,
    sibr,
    ownf,
    st,
    r1,
    r2,
    zst,
    r3,
    pm,
    sel,
    dl,
    qs,
    ps,
    ds,
    w_sem,
    h_sem,
    own_sem,
    gw_sem,
    pm_s,
    pm_r,
    hx_s,
    hx_r,
    fw_s,
    fw_r,
    sel_s,
    sel_r,
    dl_s,
    dl_r,
    sib_s,
    sib_r,
    y_s,
    y_r,
    z_s,
    z_r,
):
    k = lax.axis_index("dp")
    j = lax.axis_index("vocab")
    core = j % 2
    y = (j // 2) % 4
    zh = j // 8
    zl = k // 4
    x = k % 4

    def vid(zrel, yrel, crel):
        return ((zh + zrel) % 2) * 8 + ((y + yrel) % 4) * 2 + (core + crel) % 2

    def kid(dz, dx):
        return ((zl + dz) % 2) * 4 + (x + dx) % 4

    sibling = vid(0, 0, 1)
    up = vid(0, 1, 0)
    down = vid(0, 3, 0)
    across = vid(1, 0, 0)
    dp_steps = [(dz, dx) for dz in range(2) for dx in range(4) if (dz, dx) != (0, 0)]

    barrier = pltpu.get_barrier_semaphore()
    for dz, dx in dp_steps:
        pl.semaphore_signal(barrier, inc=1, device_id={"dp": kid(dz, dx)}, device_id_type=MESH)
    for i in range(1, NJ):
        pl.semaphore_signal(barrier, inc=1, device_id={"vocab": (j + i) % NJ}, device_id_type=MESH)

    h_copy = pltpu.make_async_copy(h_hbm, hv, h_sem)
    h_copy.start()
    w_copies = []
    for n in range(NF):
        rows = min(FC, V - n * FC)
        c = pltpu.make_async_copy(
            w_hbm.at[pl.ds(n * FC, rows), :], wv.at[pl.ds(n * FC, rows), :], w_sem.at[n]
        )
        c.start()
        w_copies.append(c)
    own_copy = pltpu.make_async_copy(
        h_hbm.at[:, pl.ds(pl.multiple_of(k * DB, DB), DB)], hx.at[k], own_sem
    )
    own_copy.start()
    wv[V:VP, :] = jnp.zeros((VP - V, D), BF)

    pad = jnp.zeros((1, VP - V), F32)
    for s in range(2):
        pm[k, s : s + 1, :] = jnp.concatenate([pos_in[s].astype(F32), pad], axis=1)
    pm[k, 2:3, 0:128] = jnp.full((1, 128), pairs[0, 0], jnp.int32).astype(F32)
    pm[k, 2:3, 128:256] = jnp.full((1, 128), pairs[0, 1], jnp.int32).astype(F32)
    pm[k, 2:3, 256:384] = jnp.full((1, 128), margins[0], F32)
    pm[k, 2:3, 384:VP] = jnp.zeros((1, VP - 384), F32)
    pm[k, 3:4, :] = jnp.zeros((1, VP), F32)

    pl.semaphore_wait(barrier, len(dp_steps) + NJ - 1)

    def to_dp(ref, ssem, rsem, i):
        dz, dx = dp_steps[i]
        return pltpu.make_async_remote_copy(
            src_ref=ref.at[k],
            dst_ref=ref.at[k],
            send_sem=ssem.at[i],
            recv_sem=rsem.at[i],
            device_id={"dp": kid(dz, dx)},
            device_id_type=MESH,
        )

    half = pl.ds(pl.multiple_of(core * L, L), L)

    def hx_copy(i):
        dz, dx = dp_steps[i]
        other = kid(dz, dx)
        return pltpu.make_async_remote_copy(
            src_ref=h_hbm.at[half, pl.ds(pl.multiple_of(other * DB, DB), DB)],
            dst_ref=hx.at[k, half, :],
            send_sem=hx_s.at[i],
            recv_sem=hx_r.at[i],
            device_id={"dp": other},
            device_id_type=MESH,
        )

    def fw_copy(i):
        dz, dx = dp_steps[i]
        src = kid(dz, 4 - dx)
        return pltpu.make_async_remote_copy(
            src_ref=hx.at[src, half, :],
            dst_ref=hx.at[src, half, :],
            send_sem=fw_s.at[i],
            recv_sem=fw_r.at[i],
            device_id={"vocab": sibling},
            device_id_type=MESH,
        )

    for i in range(7):
        to_dp(pm, pm_s, pm_r, i).start()
    for i in range(7):
        hx_copy(i).start()

    h_copy.wait()
    for n in range(NF):
        w_copies[n].wait()
        lg = lax.dot_general(
            hv[...],
            wv[n * FC : (n + 1) * FC, :],
            (((1,), (1,)), ((), ())),
            preferred_element_type=F32,
        )
        token = lax.broadcasted_iota(jnp.int32, (L, FC), 0).astype(F32)
        width = min(FC, V - n * FC)
        for s in range(2):
            spot = pm[k, s : s + 1, n * FC : (n + 1) * FC]
            picked = jnp.sum(
                jnp.where(token == spot, lg[s * L : (s + 1) * L], 0.0), axis=0, keepdims=True
            )
            b = bias[:, n * FC : n * FC + width]
            if width < FC:
                b = jnp.concatenate([b, jnp.zeros((1, FC - width), F32)], axis=1)
            valid = spot < lens[s, 0].astype(F32)
            sel[k, s : s + 1, n * FC : (n + 1) * FC] = jnp.where(
                valid, jnp.maximum(picked + b, 0.0), 0.0
            )

    for i in range(7):
        to_dp(sel, sel_s, sel_r, i).start()
    for i in range(7):
        to_dp(pm, pm_s, pm_r, i).wait()
    for i in range(7):
        to_dp(sel, sel_s, sel_r, i).wait()

    for i in range(NK):
        qs[i : i + 1, :] = sel[i, 0:1, :]
        ps[i : i + 1, :] = sel[i, 1:2, :]
    q = jnp.log1p(qs[...])
    p = jnp.log1p(ps[...])
    first = jnp.concatenate([pm[i, 2:3, 0:128] for i in range(NK)], axis=0)
    second = jnp.concatenate([pm[i, 2:3, 128:256] for i in range(NK)], axis=0)
    margin = jnp.concatenate([pm[i, 2:3, 256:384] for i in range(NK)], axis=0)

    def hit(a, b):
        return jnp.where(a == b, 1.0, 0.0)

    diff = jnp.zeros((NK, VP), F32)
    for i in range(NK):
        sign = hit(first, float(i)) - hit(second, float(i))
        diff += jnp.tile(sign, (1, VP // 128)) * p[i : i + 1, :]
    dl[j] = jnp.broadcast_to(jnp.sum(q * diff, axis=1, keepdims=True), (NK, 128))

    def dl_copy(i):
        return pltpu.make_async_remote_copy(
            src_ref=dl.at[j],
            dst_ref=dl.at[j],
            send_sem=dl_s.at[i],
            recv_sem=dl_r.at[i],
            device_id={"vocab": (j + i) % NJ},
            device_id_type=MESH,
        )

    for i in range(1, NJ):
        dl_copy(i).start()

    reg = objective_factor * regularizer_coefficient * 2.0 / NK / NK
    mean_q = reg * jnp.sum(q, axis=0, keepdims=True)
    mean_p = reg * jnp.sum(p, axis=0, keepdims=True)
    inv_q = jnp.where(qs[...] > 0.0, 1.0 / (1.0 + qs[...]), 0.0)
    inv_p = jnp.where(ps[...] > 0.0, 1.0 / (1.0 + ps[...]), 0.0)

    for i in range(1, NJ):
        dl_copy(i).wait()
    delta = dl[0]
    for i in range(1, NJ):
        delta += dl[i]
    delta = delta / logit_divisor
    weight_of = (objective_factor * 2.0 / NK / logit_divisor) * (delta - margin)
    ds[0] = (jnp.tile(weight_of, (1, VP // 128)) * diff + mean_q) * inv_q
    row = lax.broadcasted_iota(jnp.int32, (NK, 128), 0).astype(F32)
    dp = jnp.zeros((NK, VP), F32)
    for i in range(NK):
        sign = hit(first[i : i + 1, :], row) - hit(second[i : i + 1, :], row)
        dp += jnp.tile(sign * weight_of[i : i + 1, :], (1, VP // 128)) * q[i : i + 1, :]
    ds[1] = (dp + mean_p) * inv_p

    token16 = lax.broadcasted_iota(jnp.int32, (16, VP), 0).astype(F32)
    own_d = [ds[s, pl.ds(k, 1), :].astype(BF) for s in range(2)]
    own_p = [pm[k, s : s + 1, :].astype(BF) for s in range(2)]
    for crel in range(2):
        for yrel in range(4):
            for zrel in range(2):
                base = (vid(zrel, yrel, crel) * 16).astype(F32)
                token = (token16 + base).astype(BF)
                for s in range(2):
                    r = crel * 256 + yrel * 64 + zrel * 32 + s * 16
                    g[r : r + 16, :] = jnp.where(token == own_p[s], own_d[s], jnp.zeros((), BF))

    def sib_copy(c):
        return pltpu.make_async_remote_copy(
            src_ref=sibs.at[c],
            dst_ref=sibr.at[c],
            send_sem=sib_s.at[c],
            recv_sem=sib_r.at[c],
            device_id={"vocab": sibling},
            device_id_type=MESH,
        )

    def y_copy(c, which):
        src, dst, to = (
            (st.at[c, 128:192, 0:HA], r1.at[c, 0], up),
            (st.at[c, 128:192, HA:HC], r1.at[c, 1], down),
            (st.at[c, 64:128, HA:HC], r2.at[c, 0, :, HA:HC], up),
            (st.at[c, 192:256, 0:HA], r2.at[c, 1, :, 0:HA], down),
            (st.at[c, 64:128, 0:HA], r2.at[c, 0, :, 0:HA], up),
            (st.at[c, 192:256, HA:HC], r2.at[c, 1, :, HA:HC], down),
        )[which]
        return pltpu.make_async_remote_copy(
            src_ref=src,
            dst_ref=dst,
            send_sem=y_s.at[c, which],
            recv_sem=y_r.at[c, which],
            device_id={"vocab": to},
            device_id_type=MESH,
        )

    def z_copy(c):
        return pltpu.make_async_remote_copy(
            src_ref=zst.at[c],
            dst_ref=r3.at[c],
            send_sem=z_s.at[c],
            recv_sem=z_r.at[c],
            device_id={"vocab": across},
            device_id_type=MESH,
        )

    def pair_sum(c, rows, cols):
        return ownf[c, rows, cols] + sibr[c, rows, cols].astype(F32)

    lo, hi, both = slice(0, HA), slice(HA, HC), slice(0, HC)

    def stage1(c):
        sib_copy(c).wait_recv()
        st[c, 128:192, :] = pair_sum(c, slice(128, 192), both).astype(BF)
        y_copy(c, 0).start()
        y_copy(c, 1).start()
        st[c, 64:128, hi] = pair_sum(c, slice(64, 128), hi).astype(BF)
        y_copy(c, 2).start()
        st[c, 192:256, lo] = pair_sum(c, slice(192, 256), lo).astype(BF)
        y_copy(c, 3).start()

    def stage2(c):
        y_copy(c, 0).wait_recv()
        st[c, 64:128, lo] = (pair_sum(c, slice(64, 128), lo) + r1[c, 0].astype(F32)).astype(BF)
        y_copy(c, 4).start()
        y_copy(c, 1).wait_recv()
        st[c, 192:256, hi] = (pair_sum(c, slice(192, 256), hi) + r1[c, 1].astype(F32)).astype(BF)
        y_copy(c, 5).start()

    def stage3(c):
        for which in (2, 3, 4, 5):
            y_copy(c, which).wait_recv()
        far = slice(32, 64)
        zst[c] = (
            pair_sum(c, far, both) + r2[c, 0, far].astype(F32) + r2[c, 1, far].astype(F32)
        ).astype(BF)
        z_copy(c).start()
        near = slice(0, 32)
        ownf[c, near, :] = (
            pair_sum(c, near, both) + r2[c, 0, near].astype(F32) + r2[c, 1, near].astype(F32)
        )

    def stage4(c):
        z_copy(c).wait_recv()
        total = (ownf[c, 0:32, :] + r3[c].astype(F32)).astype(BF)
        cols = pl.ds(pl.multiple_of(c * HC, HC), HC)
        gh_out[0, :, cols] = total[0:16]
        gh_out[1, :, cols] = total[16:32]

    def when(cond):
        return pl.when(cond)

    def gh_step(c, carry):
        cols = pl.ds(pl.multiple_of(c * HC, HC), HC)
        part = jnp.dot(g[...], wv[:, cols], preferred_element_type=F32)
        sibs[c] = part[256:512].astype(BF)
        sib_copy(c).start()
        ownf[c] = part[0:256]

        @when(c >= 1)
        def _():
            stage1(c - 1)

        @when(c >= 4)
        def _():
            stage2(c - 4)

        return carry

    lax.fori_loop(0, NH, gh_step, 0)
    stage1(NH - 1)

    for i in range(7):
        hx_copy(i).wait_recv()
        fw_copy(i).start()
    own_copy.wait()
    for i in range(7):
        fw_copy(i).wait_recv()

    token256 = lax.broadcasted_iota(jnp.int32, (L, WC), 0).astype(F32).astype(BF)

    def gw_copy(n, slot, rows):
        return pltpu.make_async_copy(
            gwst.at[slot, 0:rows, :],
            gw_out.at[pl.ds(pl.multiple_of(n * WC, WC), rows), :],
            gw_sem.at[slot],
        )

    tail = V - (NW - 1) * WC

    def gw_step(n, carry):
        slot = n % 2
        cols = pl.ds(pl.multiple_of(n * WC, WC), WC)
        for i in range(NK):
            for s in range(2):
                spot = pm[i, s : s + 1, cols].astype(BF)
                val = ds[s, i : i + 1, cols].astype(BF)
                r = (i * 2 + s) * L
                gc[r : r + L, :] = jnp.where(token256 == spot, val, jnp.zeros((), BF))
        out = lax.dot_general(
            gc[...],
            hx[...].reshape(NK * 2 * L, DB),
            (((0,), (0,)), ((), ())),
            preferred_element_type=F32,
        )

        @when(n >= 2)
        def _():
            gw_copy(n - 2, slot, WC).wait()

        gwst[slot] = out

        @when(n < NW - 1)
        def _():
            gw_copy(n, slot, WC).start()

        @when(n == NW - 1)
        def _():
            gw_copy(n, slot, tail).start()

        @when(n < 2)
        def _():
            stage2(4 + 2 * n)
            stage2(5 + 2 * n)

        stage3(2 * n)
        stage3(2 * n + 1)

        @when(n >= 1)
        def _():
            stage4(2 * n - 2)
            stage4(2 * n - 1)

        return carry

    lax.fori_loop(0, NW, gw_step, 0)
    stage4(NH - 2)
    stage4(NH - 1)

    gw_copy(NW - 2, (NW - 2) % 2, WC).wait()
    gw_copy(NW - 1, (NW - 1) % 2, tail).wait()
    for i in range(7):
        hx_copy(i).wait_send()
        fw_copy(i).wait_send()

    def drain(c, carry):
        sib_copy(c).wait_send()
        for which in range(6):
            y_copy(c, which).wait_send()
        z_copy(c).wait_send()
        return carry

    lax.fori_loop(0, NH, drain, 0)


def local(hidden, weight, bias, positions, lengths, pairs, margins):
    vmem = pl.BlockSpec(memory_space=pltpu.VMEM)
    smem = pl.BlockSpec(memory_space=pltpu.SMEM)
    hbm = pl.BlockSpec(memory_space=pl.ANY)
    dma = pltpu.SemaphoreType.DMA
    scratch = [
        pltpu.VMEM((VP, D), BF),
        pltpu.VMEM((2 * L, D), BF),
        pltpu.VMEM((NK, 2 * L, DB), BF),
        pltpu.VMEM((2 * L, VP), BF),
        pltpu.VMEM((NK * 2 * L, WC), BF),
        pltpu.VMEM((2, WC, DB), F32),
        pltpu.VMEM((NH, 256, HC), BF),
        pltpu.VMEM((NH, 256, HC), BF),
        pltpu.VMEM((NH, 256, HC), F32),
        pltpu.VMEM((NH, 256, HC), BF),
        pltpu.VMEM((NH, 2, 64, HA), BF),
        pltpu.VMEM((NH, 2, 64, HC), BF),
        pltpu.VMEM((NH, 32, HC), BF),
        pltpu.VMEM((NH, 32, HC), BF),
        pltpu.VMEM((NK, 4, VP), F32),
        pltpu.VMEM((NK, 2, VP), F32),
        pltpu.VMEM((NJ, NK, 128), F32),
        pltpu.VMEM((NK, VP), F32),
        pltpu.VMEM((NK, VP), F32),
        pltpu.VMEM((2, NK, VP), F32),
        dma((NF,)),
        dma,
        dma,
        dma((2,)),
        dma((7,)),
        dma((7,)),
        dma((7,)),
        dma((7,)),
        dma((7,)),
        dma((7,)),
        dma((7,)),
        dma((7,)),
        dma((NJ,)),
        dma((NJ,)),
        dma((NH,)),
        dma((NH,)),
        dma((NH, 6)),
        dma((NH, 6)),
        dma((NH,)),
        dma((NH,)),
    ]
    gh, gw = pl.pallas_call(
        kernel,
        out_shape=(
            jax.ShapeDtypeStruct((2, 16, D), BF),
            jax.ShapeDtypeStruct((V, DB), F32),
        ),
        in_specs=[hbm, hbm, vmem, vmem, smem, smem, smem],
        out_specs=(vmem, hbm),
        scratch_shapes=scratch,
        compiler_params=pltpu.CompilerParams(
            collective_id=0, has_side_effects=True, vmem_limit_bytes=62 * 2**20
        ),
        cost_estimate=pl.CostEstimate(
            flops=6 * 512 * V * D, bytes_accessed=24 * 2**20, transcendentals=0
        ),
        name="splade_backward",
    )(
        hidden.reshape(2 * L, D),
        weight,
        bias.reshape(1, V),
        positions,
        lengths,
        pairs,
        margins,
    )
    return gh.reshape(2, 1, 16, D), gw


def solution(mesh):
    in_specs = (
        P(None, "dp", None, None),
        P("vocab", None),
        P("vocab"),
        P(None, "dp", "vocab"),
        P(None, "dp"),
        P("dp", None),
        P("dp"),
    )
    out_specs = (P(None, "dp", "vocab", None), P("vocab", "dp"))
    return jax.shard_map(local, mesh=mesh, in_specs=in_specs, out_specs=out_specs, check_vma=False)
```

```python
import jax
import jax.numpy as jnp
from jax import lax
from jax.experimental import pallas as pl
from jax.experimental.pallas import tpu as pltpu
from jax.sharding import PartitionSpec as P

logit_divisor = 16.0
objective_factor = 256.0
regularizer_coefficient = 0.1

BF = jnp.bfloat16
F32 = jnp.float32
MESH = pl.DeviceIdType.MESH

V = 2000
VP = 2048
D = 4096
L = 256
NK = 8
NJ = 16
DB = 512
FWD = ((0, 256), (256, 256), (512, 512), (1024, 512), (1536, 512))
NF = len(FWD)
HC = 512
NH = D // HC
HA = HC // 2
WC = 512
NW = VP // WC
CP = 5


def kernel(
    h_hbm,
    w_hbm,
    bias,
    pos_in,
    lens,
    pairs,
    margins,
    gh_out,
    gw_out,
    wv,
    hv,
    hx,
    g,
    gc,
    gwst,
    sibs,
    sibr,
    ownf,
    st,
    r1,
    r2,
    zst,
    r3,
    pm,
    sel,
    dl,
    qs,
    ps,
    ds,
    w_sem,
    h_sem,
    own_sem,
    gw_sem,
    pm_s,
    pm_r,
    hx_s,
    hx_r,
    fw_s,
    fw_r,
    sel_s,
    sel_r,
    dl_s,
    dl_r,
    sib_s,
    sib_r,
    y_s,
    y_r,
    z_s,
    z_r,
):
    k = lax.axis_index("dp")
    j = lax.axis_index("vocab")
    core = j % 2
    y = (j // 2) % 4
    zh = j // 8
    zl = k // 4
    x = k % 4

    def vid(zrel, yrel, crel):
        return ((zh + zrel) % 2) * 8 + ((y + yrel) % 4) * 2 + (core + crel) % 2

    def kid(dz, dx):
        return ((zl + dz) % 2) * 4 + (x + dx) % 4

    sibling = vid(0, 0, 1)
    up = vid(0, 1, 0)
    down = vid(0, 3, 0)
    across = vid(1, 0, 0)
    dp_steps = [(dz, dx) for dz in range(2) for dx in range(4) if (dz, dx) != (0, 0)]

    barrier = pltpu.get_barrier_semaphore()
    for dz, dx in dp_steps:
        pl.semaphore_signal(barrier, inc=1, device_id={"dp": kid(dz, dx)}, device_id_type=MESH)
    for dx in range(4):
        pl.semaphore_signal(
            barrier,
            inc=1,
            device_id={"dp": kid(1, dx), "vocab": across},
            device_id_type=MESH,
        )
    for i in range(1, NJ):
        pl.semaphore_signal(barrier, inc=1, device_id={"vocab": (j + i) % NJ}, device_id_type=MESH)

    h_copy = pltpu.make_async_copy(h_hbm, hv, h_sem)
    h_copy.start()
    w_copies = []
    for n, (at, size) in enumerate(FWD):
        rows = min(size, V - at)
        c = pltpu.make_async_copy(
            w_hbm.at[pl.ds(at, rows), :], wv.at[pl.ds(at, rows), :], w_sem.at[n]
        )
        w_copies.append(c)
    w_copies[0].start()
    w_copies[1].start()
    own_copy = pltpu.make_async_copy(
        hv.at[core, :, :, :, pl.ds(pl.multiple_of(k * DB, DB), DB)],
        hx.at[k, core],
        own_sem,
    )
    wv[V:VP, :] = jnp.zeros((VP - V, D), BF)

    pad = jnp.zeros((1, VP - V), F32)
    for s in range(2):
        pm[k, s : s + 1, :] = jnp.concatenate([pos_in[s].astype(F32), pad], axis=1)
    pm[k, 2:3, 0:128] = jnp.full((1, 128), pairs[0], jnp.int32).astype(F32)
    pm[k, 2:3, 128:256] = jnp.full((1, 128), pairs[1], jnp.int32).astype(F32)
    pm[k, 2:3, 256:384] = jnp.full((1, 128), margins[0], F32)
    pm[k, 2:3, 384:VP] = jnp.zeros((1, VP - 384), F32)
    pm[k, 3:4, :] = jnp.zeros((1, VP), F32)

    def to_dp(ref, ssem, rsem, i):
        dz, dx = dp_steps[i]
        return pltpu.make_async_remote_copy(
            src_ref=ref.at[k],
            dst_ref=ref.at[k],
            send_sem=ssem.at[i],
            recv_sem=rsem.at[i],
            device_id={"dp": kid(dz, dx)},
            device_id_type=MESH,
        )

    near = [(i, None, None) for i in range(7) if dp_steps[i][0] == 0]
    far = [
        [(i, part, sub) for i in range(7) if dp_steps[i][0] == 1 for part in range(2)]
        for sub in range(2)
    ]

    def hx_copy(i, part, sub):
        dz, dx = dp_steps[i]
        other = kid(dz, dx)
        cols = pl.ds(pl.multiple_of(other * DB, DB), DB)
        if part is None:
            src, dst, sems = hv.at[core, :, :, :, cols], hx.at[k, core], (i, 0, 0)
            to = {"dp": other}
        else:
            src, dst = hv.at[core, part, sub, :, cols], hx.at[k, core, part, sub]
            sems, to = (i, part, sub), {"dp": other, "vocab": vid(part, 0, 0)}
        return pltpu.make_async_remote_copy(
            src_ref=src,
            dst_ref=dst,
            send_sem=hx_s.at[sems],
            recv_sem=hx_r.at[sems],
            device_id=to,
            device_id_type=MESH,
        )

    def fw_copy(which):
        if which == 0:
            ref = hx.at[pl.ds(zl * 4, 4), core]
        else:
            ref = hx.at[pl.ds((1 - zl) * 4, 4), core, :, which - 1]
        return pltpu.make_async_remote_copy(
            src_ref=ref,
            dst_ref=ref,
            send_sem=fw_s.at[which],
            recv_sem=fw_r.at[which],
            device_id={"vocab": sibling},
            device_id_type=MESH,
        )

    def pass_on(which):
        if which == 0:
            own_copy.wait()
            batch = near
        else:
            batch = far[which - 1]
        for item in batch:
            hx_copy(*item).wait_recv()
        fw_copy(which).start()

    h_copy.wait()
    for n, (at, size) in enumerate(FWD):
        w_copies[n].wait()
        if n + 2 < NF:
            w_copies[n + 2].start()
        lg = lax.dot_general(
            hv[...].reshape(2 * L, D),
            wv[at : at + size, :],
            (((1,), (1,)), ((), ())),
            preferred_element_type=F32,
        )
        token = lax.broadcasted_iota(jnp.int32, (L, size), 0).astype(F32)
        width = min(size, V - at)
        for s in range(2):
            spot = pm[k, s : s + 1, at : at + size]
            picked = jnp.sum(
                jnp.where(token == spot, lg[s * L : (s + 1) * L], 0.0), axis=0, keepdims=True
            )
            b = bias[:, at : at + width]
            if width < size:
                b = jnp.concatenate([b, jnp.zeros((1, size - width), F32)], axis=1)
            valid = spot < lens[s].astype(F32)
            sel[k, s : s + 1, at : at + size] = jnp.where(valid, jnp.maximum(picked + b, 0.0), 0.0)
        if n == 1:
            pl.semaphore_wait(barrier, len(dp_steps) + 4 + NJ - 1)
            for i in range(7):
                to_dp(pm, pm_s, pm_r, i).start()
            for item in far[0]:
                hx_copy(*item).start()
            own_copy.start()

    for i in range(7):
        to_dp(sel, sel_s, sel_r, i).start()
    for i in range(7):
        to_dp(pm, pm_s, pm_r, i).wait()
    for i in range(7):
        to_dp(sel, sel_s, sel_r, i).wait()
    for item in near:
        hx_copy(*item).start()

    for i in range(NK):
        qs[i : i + 1, :] = sel[i, 0:1, :]
        ps[i : i + 1, :] = sel[i, 1:2, :]
    q = jnp.log1p(qs[...])
    p = jnp.log1p(ps[...])
    first = jnp.concatenate([pm[i, 2:3, 0:128] for i in range(NK)], axis=0)
    second = jnp.concatenate([pm[i, 2:3, 128:256] for i in range(NK)], axis=0)
    margin = jnp.concatenate([pm[i, 2:3, 256:384] for i in range(NK)], axis=0)

    def hit(a, b):
        return jnp.where(a == b, 1.0, 0.0)

    diff = jnp.zeros((NK, VP), F32)
    for i in range(NK):
        sign = hit(first, float(i)) - hit(second, float(i))
        diff += jnp.tile(sign, (1, VP // 128)) * p[i : i + 1, :]
    dl[j] = jnp.broadcast_to(jnp.sum(q * diff, axis=1, keepdims=True), (NK, 128))

    def dl_copy(i):
        return pltpu.make_async_remote_copy(
            src_ref=dl.at[j],
            dst_ref=dl.at[j],
            send_sem=dl_s.at[i],
            recv_sem=dl_r.at[i],
            device_id={"vocab": (j + i) % NJ},
            device_id_type=MESH,
        )

    for i in range(1, NJ):
        dl_copy(i).start()

    reg = objective_factor * regularizer_coefficient * 2.0 / NK / NK
    mean_q = reg * jnp.sum(q, axis=0, keepdims=True)
    mean_p = reg * jnp.sum(p, axis=0, keepdims=True)
    inv_q = jnp.where(qs[...] > 0.0, 1.0 / (1.0 + qs[...]), 0.0)
    inv_p = jnp.where(ps[...] > 0.0, 1.0 / (1.0 + ps[...]), 0.0)

    for i in range(1, NJ):
        dl_copy(i).wait()
    delta = dl[0]
    for i in range(1, NJ):
        delta += dl[i]
    delta = delta / logit_divisor
    weight_of = (objective_factor * 2.0 / NK / logit_divisor) * (delta - margin)
    ds[0] = (jnp.tile(weight_of, (1, VP // 128)) * diff + mean_q) * inv_q
    row = lax.broadcasted_iota(jnp.int32, (NK, 128), 0).astype(F32)
    dp = jnp.zeros((NK, VP), F32)
    for i in range(NK):
        sign = hit(first[i : i + 1, :], row) - hit(second[i : i + 1, :], row)
        dp += jnp.tile(sign * weight_of[i : i + 1, :], (1, VP // 128)) * q[i : i + 1, :]
    ds[1] = (dp + mean_p) * inv_p

    token16 = lax.broadcasted_iota(jnp.int32, (16, VP), 0).astype(F32)
    own_d = [ds[s, pl.ds(k, 1), :].astype(BF) for s in range(2)]
    own_p = [pm[k, s : s + 1, :].astype(BF) for s in range(2)]
    for crel in range(2):
        for yrel in range(4):
            for zrel in range(2):
                base = (vid(zrel, yrel, crel) * 16).astype(F32)
                token = (token16 + base).astype(BF)
                for s in range(2):
                    r = crel * 256 + yrel * 64 + zrel * 32 + s * 16
                    g[r : r + 16, :] = jnp.where(token == own_p[s], own_d[s], jnp.zeros((), BF))

    def sib_copy(c):
        return pltpu.make_async_remote_copy(
            src_ref=sibs.at[c],
            dst_ref=sibr.at[c],
            send_sem=sib_s.at[c],
            recv_sem=sib_r.at[c],
            device_id={"vocab": sibling},
            device_id_type=MESH,
        )

    def y_copy(c, which):
        src, dst, to = (
            (st.at[c, 128:192, 0:HA], r1.at[c, 0], up),
            (st.at[c, 128:192, HA:HC], r1.at[c, 1], down),
            (st.at[c, 64:128, HA:HC], r2.at[c, 0, :, HA:HC], up),
            (st.at[c, 192:256, 0:HA], r2.at[c, 1, :, 0:HA], down),
            (st.at[c, 64:128, 0:HA], r2.at[c, 0, :, 0:HA], up),
            (st.at[c, 192:256, HA:HC], r2.at[c, 1, :, HA:HC], down),
        )[which]
        return pltpu.make_async_remote_copy(
            src_ref=src,
            dst_ref=dst,
            send_sem=y_s.at[c, which],
            recv_sem=y_r.at[c, which],
            device_id={"vocab": to},
            device_id_type=MESH,
        )

    def z_copy(c):
        return pltpu.make_async_remote_copy(
            src_ref=zst.at[c],
            dst_ref=r3.at[c],
            send_sem=z_s.at[c],
            recv_sem=z_r.at[c],
            device_id={"vocab": across},
            device_id_type=MESH,
        )

    def pair_sum(c, rows, cols):
        return ownf[c, rows, cols] + sibr[c, rows, cols].astype(F32)

    lo, hi, both = slice(0, HA), slice(HA, HC), slice(0, HC)

    def stage1(c):
        sib_copy(c).wait_recv()
        st[c, 128:192, :] = pair_sum(c, slice(128, 192), both).astype(BF)
        y_copy(c, 0).start()
        y_copy(c, 1).start()
        st[c, 64:128, hi] = pair_sum(c, slice(64, 128), hi).astype(BF)
        y_copy(c, 2).start()
        st[c, 192:256, lo] = pair_sum(c, slice(192, 256), lo).astype(BF)
        y_copy(c, 3).start()

    def stage2(c):
        y_copy(c, 0).wait_recv()
        st[c, 64:128, lo] = (pair_sum(c, slice(64, 128), lo) + r1[c, 0].astype(F32)).astype(BF)
        y_copy(c, 4).start()
        y_copy(c, 1).wait_recv()
        st[c, 192:256, hi] = (pair_sum(c, slice(192, 256), hi) + r1[c, 1].astype(F32)).astype(BF)
        y_copy(c, 5).start()

    def stage3(c):
        for which in (2, 3, 4, 5):
            y_copy(c, which).wait_recv()
        away = slice(32, 64)
        zst[c] = (
            pair_sum(c, away, both) + r2[c, 0, away].astype(F32) + r2[c, 1, away].astype(F32)
        ).astype(BF)
        z_copy(c).start()
        here = slice(0, 32)
        ownf[c, here, :] = (
            pair_sum(c, here, both) + r2[c, 0, here].astype(F32) + r2[c, 1, here].astype(F32)
        )

    def stage4(c):
        z_copy(c).wait_recv()
        total = (ownf[c, 0:32, :] + r3[c].astype(F32)).astype(BF)
        cols = pl.ds(pl.multiple_of(c * HC, HC), HC)
        gh_out[0, :, cols] = total[0:16]
        gh_out[1, :, cols] = total[16:32]

    def when(cond):
        return pl.when(cond)

    def gh_step(c, carry):
        cols = pl.ds(pl.multiple_of(c * HC, HC), HC)
        part = jnp.dot(g[...], wv[:, cols], preferred_element_type=F32)
        sibs[c] = part[256:512].astype(BF)
        sib_copy(c).start()
        ownf[c] = part[0:256]

        @when(c >= 1)
        def _():
            stage1(c - 1)

        @when(c >= 4)
        def _():
            stage2(c - 4)

        @when(c == 0)
        def _():
            for item in far[1]:
                hx_copy(*item).start()

        @when(c == 2)
        def _():
            pass_on(1)

        @when(c == 7)
        def _():
            pass_on(0)

        return carry

    lax.fori_loop(0, NH, gh_step, 0)
    stage1(NH - 1)

    pass_on(2)
    for which in range(3):
        fw_copy(which).wait_recv()

    token256 = lax.broadcasted_iota(jnp.int32, (L, WC), 0).astype(F32).astype(BF)

    def gw_copy(n, slot, rows):
        return pltpu.make_async_copy(
            gwst.at[slot, 0:rows, :],
            gw_out.at[pl.ds(pl.multiple_of(n * WC, WC), rows), :],
            gw_sem.at[slot],
        )

    tail = V - (NW - 1) * WC

    def gw_step(n, carry):
        slot = n % 2
        cols = pl.ds(pl.multiple_of(n * WC, WC), WC)
        for i in range(NK):
            for s in range(2):
                spot = pm[i, s : s + 1, cols].astype(BF)
                val = ds[s, i : i + 1, cols].astype(BF)
                r = (i * 2 + s) * L
                gc[r : r + L, :] = jnp.where(token256 == spot, val, jnp.zeros((), BF))
        out = lax.dot_general(
            gc[...],
            hx[...].reshape(NK * 2 * L, DB),
            (((0,), (0,)), ((), ())),
            preferred_element_type=F32,
        )

        @when(n >= 2)
        def _():
            gw_copy(n - 2, slot, WC).wait()

        gwst[slot] = out

        @when(n < NW - 1)
        def _():
            gw_copy(n, slot, WC).start()

        @when(n == NW - 1)
        def _():
            gw_copy(n, slot, tail).start()

        @when(n < 2)
        def _():
            stage2(4 + 2 * n)
            stage2(5 + 2 * n)

        stage3(2 * n)
        stage3(2 * n + 1)

        @when(n >= 1)
        def _():
            stage4(2 * n - 2)
            stage4(2 * n - 1)

        return carry

    lax.fori_loop(0, NW, gw_step, 0)
    stage4(NH - 2)
    stage4(NH - 1)

    gw_copy(NW - 2, (NW - 2) % 2, WC).wait()
    gw_copy(NW - 1, (NW - 1) % 2, tail).wait()
    for item in near + far[0] + far[1]:
        hx_copy(*item).wait_send()
    for which in range(3):
        fw_copy(which).wait_send()

    def drain(c, carry):
        sib_copy(c).wait_send()
        for which in range(6):
            y_copy(c, which).wait_send()
        z_copy(c).wait_send()
        return carry

    lax.fori_loop(0, NH, drain, 0)


def finish(gh_in, gw_in, gh_out, gw_out, gh_v, gw_v, in_sem, out_sem):
    ins = [pltpu.make_async_copy(gh_in, gh_v, in_sem.at[CP])]
    outs = [pltpu.make_async_copy(gh_v, gh_out, out_sem.at[CP])]
    for i in range(CP):
        rows = pl.ds(i * (V // CP), V // CP)
        ins.append(pltpu.make_async_copy(gw_in.at[rows, :], gw_v.at[rows, :], in_sem.at[i]))
        outs.append(pltpu.make_async_copy(gw_v.at[rows, :], gw_out.at[rows, :], out_sem.at[i]))
    for c in ins:
        c.start()
    for a, b in zip(ins, outs):
        a.wait()
        b.start()
    for c in outs:
        c.wait()


def local(hidden, weight, bias, positions, lengths, pairs, margins):
    vmem = pl.BlockSpec(memory_space=pltpu.VMEM)
    smem = pl.BlockSpec(memory_space=pltpu.SMEM)
    hbm = pl.BlockSpec(memory_space=pl.ANY)
    dma = pltpu.SemaphoreType.DMA
    scratch = [
        pltpu.VMEM((VP, D), BF),
        pltpu.VMEM((2, 2, 2, L // 4, D), BF),
        pltpu.VMEM((NK, 2, 2, 2, L // 4, DB), BF),
        pltpu.VMEM((2 * L, VP), BF),
        pltpu.VMEM((NK * 2 * L, WC), BF),
        pltpu.VMEM((2, WC, DB), F32),
        pltpu.VMEM((NH, 256, HC), BF),
        pltpu.VMEM((NH, 256, HC), BF),
        pltpu.VMEM((NH, 256, HC), F32),
        pltpu.VMEM((NH, 256, HC), BF),
        pltpu.VMEM((NH, 2, 64, HA), BF),
        pltpu.VMEM((NH, 2, 64, HC), BF),
        pltpu.VMEM((NH, 32, HC), BF),
        pltpu.VMEM((NH, 32, HC), BF),
        pltpu.VMEM((NK, 4, VP), F32),
        pltpu.VMEM((NK, 2, VP), F32),
        pltpu.VMEM((NJ, NK, 128), F32),
        pltpu.VMEM((NK, VP), F32),
        pltpu.VMEM((NK, VP), F32),
        pltpu.VMEM((2, NK, VP), F32),
        dma((NF,)),
        dma,
        dma,
        dma((2,)),
        dma((7,)),
        dma((7,)),
        dma((7, 2, 2)),
        dma((7, 2, 2)),
        dma((3,)),
        dma((3,)),
        dma((7,)),
        dma((7,)),
        dma((NJ,)),
        dma((NJ,)),
        dma((NH,)),
        dma((NH,)),
        dma((NH, 6)),
        dma((NH, 6)),
        dma((NH,)),
        dma((NH,)),
    ]
    gh, gw = pl.pallas_call(
        kernel,
        out_shape=(
            jax.ShapeDtypeStruct((2, 16, D), BF),
            jax.ShapeDtypeStruct((V, DB), F32),
        ),
        in_specs=[hbm, hbm, vmem, vmem, smem, smem, smem],
        out_specs=(vmem, hbm),
        scratch_shapes=scratch,
        compiler_params=pltpu.CompilerParams(
            collective_id=0, has_side_effects=True, vmem_limit_bytes=62 * 2**20
        ),
        cost_estimate=pl.CostEstimate(
            flops=6 * 512 * V * D, bytes_accessed=24 * 2**20, transcendentals=0
        ),
        name="splade_backward",
    )(
        hidden.reshape(2, 2, 2, L // 4, D),
        weight,
        bias.reshape(1, V),
        positions,
        lengths.reshape(2),
        pairs.reshape(2),
        margins,
    )
    gh, gw = pl.pallas_call(
        finish,
        out_shape=(
            jax.ShapeDtypeStruct((2, 16, D), BF),
            jax.ShapeDtypeStruct((V, DB), F32),
        ),
        in_specs=[hbm, hbm],
        out_specs=(hbm, hbm),
        scratch_shapes=[
            pltpu.VMEM((2, 16, D), BF),
            pltpu.VMEM((V, DB), F32),
            dma((CP + 1,)),
            dma((CP + 1,)),
        ],
        compiler_params=pltpu.CompilerParams(vmem_limit_bytes=62 * 2**20),
        name="finish",
    )(gh, gw)
    return gh.reshape(2, 1, 16, D), gw


def solution(mesh):
    in_specs = (
        P(None, "dp", None, None),
        P("vocab", None),
        P("vocab"),
        P(None, "dp", "vocab"),
        P(None, "dp"),
        P("dp", None),
        P("dp"),
    )
    out_specs = (P(None, "dp", "vocab", None), P("vocab", "dp"))
    return jax.shard_map(local, mesh=mesh, in_specs=in_specs, out_specs=out_specs, check_vma=False)
```

```python
import jax
import jax.numpy as jnp
from jax import lax
from jax.experimental import pallas as pl
from jax.experimental.pallas import tpu as pltpu
from jax.sharding import PartitionSpec as P

logit_divisor = 16.0
objective_factor = 256.0
regularizer_coefficient = 0.1

BF = jnp.bfloat16
F32 = jnp.float32
MESH = pl.DeviceIdType.MESH

V = 2000
VP = 2048
D = 4096
L = 256
NK = 8
NJ = 16
DB = 512
FWD = ((0, 256), (256, 256), (512, 512), (1024, 1024))
NF = len(FWD)
HC = 512
NH = D // HC
WC = 512
NW = VP // WC
ZFIRST = (0, 3, 7)
TURN = (0, 1, 0, 1, 1, 0, 1, 0)
FORTH, BACK = (64, 192), (192, 64)
PLAN = {
    2: ((0, 1),),
    3: ((1, 1),),
    4: ((2, 1),),
    5: ((3, 1),),
    6: ((1, 2), (4, 1), (5, 1)),
    7: ((0, 2), (2, 2)),
    8: ((1, 3), (6, 1), (7, 1)),
    9: ((3, 2), (4, 2), (5, 2)),
    10: ((0, 3),),
    11: ((1, 4), (2, 3), (6, 2)),
    12: ((3, 3), (7, 2)),
    13: ((0, 4), (4, 3), (5, 3)),
    14: ((2, 4), (3, 4), (6, 3), (7, 3)),
    15: ((4, 4), (5, 4), (7, 4), (6, 4)),
}


def kernel(
    h_hbm,
    w_hbm,
    bias,
    pos_in,
    lens,
    pairs,
    margins,
    gh_out,
    gw_out,
    wv,
    hv,
    hx,
    g,
    gc,
    sibs,
    sibr,
    ownf,
    st,
    r1,
    r2,
    zst,
    r3,
    pm,
    sel,
    dl,
    qs,
    ps,
    ds,
    w_sem,
    h_sem,
    own_sem,
    pm_s,
    pm_r,
    hx_s,
    hx_r,
    fw_s,
    fw_r,
    sel_s,
    sel_r,
    dl_s,
    dl_r,
    sib_s,
    sib_r,
    y_s,
    y_r,
    z_s,
    z_r,
):
    k = lax.axis_index("dp")
    j = lax.axis_index("vocab")
    core = j % 2
    y = (j // 2) % 4
    zh = j // 8
    zl = k // 4
    x = k % 4

    def vid(zrel, yrel, crel):
        return ((zh + zrel) % 2) * 8 + ((y + yrel) % 4) * 2 + (core + crel) % 2

    def kid(dz, dx):
        return ((zl + dz) % 2) * 4 + (x + dx) % 4

    sibling = vid(0, 0, 1)
    up = vid(0, 1, 0)
    down = vid(0, 3, 0)
    across = vid(1, 0, 0)
    dp_steps = [(dz, dx) for dz in range(2) for dx in range(4) if (dz, dx) != (0, 0)]

    barrier = pltpu.get_barrier_semaphore()
    for dz, dx in dp_steps:
        pl.semaphore_signal(barrier, inc=1, device_id={"dp": kid(dz, dx)}, device_id_type=MESH)
    for dx in range(4):
        pl.semaphore_signal(
            barrier,
            inc=1,
            device_id={"dp": kid(1, dx), "vocab": across},
            device_id_type=MESH,
        )
    for i in range(1, NJ):
        pl.semaphore_signal(barrier, inc=1, device_id={"vocab": (j + i) % NJ}, device_id_type=MESH)

    h_copy = pltpu.make_async_copy(h_hbm, hv, h_sem)
    h_copy.start()
    w_copies = []
    for n, (at, size) in enumerate(FWD):
        rows = min(size, V - at)
        c = pltpu.make_async_copy(
            w_hbm.at[pl.ds(at, rows), :], wv.at[pl.ds(at, rows), :], w_sem.at[n]
        )
        w_copies.append(c)
    w_copies[0].start()
    w_copies[1].start()
    own_copy = pltpu.make_async_copy(
        hv.at[core, :, :, :, pl.ds(pl.multiple_of(k * DB, DB), DB)],
        hx.at[k, core],
        own_sem,
    )
    wv[V:VP, :] = jnp.zeros((VP - V, D), BF)

    pad = jnp.zeros((1, VP - V), F32)
    for s in range(2):
        pm[k, s : s + 1, :] = jnp.concatenate([pos_in[s].astype(F32), pad], axis=1)
    pm[k, 2:3, 0:128] = jnp.full((1, 128), pairs[0], jnp.int32).astype(F32)
    pm[k, 2:3, 128:256] = jnp.full((1, 128), pairs[1], jnp.int32).astype(F32)
    pm[k, 2:3, 256:384] = jnp.full((1, 128), margins[0], F32)
    pm[k, 2:3, 384:VP] = jnp.zeros((1, VP - 384), F32)
    pm[k, 3:4, :] = jnp.zeros((1, VP), F32)

    def to_dp(ref, ssem, rsem, i):
        dz, dx = dp_steps[i]
        return pltpu.make_async_remote_copy(
            src_ref=ref.at[k],
            dst_ref=ref.at[k],
            send_sem=ssem.at[i],
            recv_sem=rsem.at[i],
            device_id={"dp": kid(dz, dx)},
            device_id_type=MESH,
        )

    near = [(i, None, None) for i in range(7) if dp_steps[i][0] == 0]
    far = [
        [(i, part, sub) for i in range(7) if dp_steps[i][0] == 1 for part in range(2)]
        for sub in range(2)
    ]

    def hx_copy(i, part, sub):
        dz, dx = dp_steps[i]
        other = kid(dz, dx)
        cols = pl.ds(pl.multiple_of(other * DB, DB), DB)
        if part is None:
            src, dst, sems = hv.at[core, :, :, :, cols], hx.at[k, core], (i, 0, 0)
            to = {"dp": other}
        else:
            src, dst = hv.at[core, part, sub, :, cols], hx.at[k, core, part, sub]
            sems, to = (i, part, sub), {"dp": other, "vocab": vid(part, 0, 0)}
        return pltpu.make_async_remote_copy(
            src_ref=src,
            dst_ref=dst,
            send_sem=hx_s.at[sems],
            recv_sem=hx_r.at[sems],
            device_id=to,
            device_id_type=MESH,
        )

    def fw_copy(which):
        if which == 0:
            ref = hx.at[pl.ds(zl * 4, 4), core]
        else:
            ref = hx.at[pl.ds((1 - zl) * 4, 4), core, :, which - 1]
        return pltpu.make_async_remote_copy(
            src_ref=ref,
            dst_ref=ref,
            send_sem=fw_s.at[which],
            recv_sem=fw_r.at[which],
            device_id={"vocab": sibling},
            device_id_type=MESH,
        )

    def pass_on(which):
        if which == 0:
            own_copy.wait()
            batch = near
        else:
            batch = far[which - 1]
        for item in batch:
            hx_copy(*item).wait_recv()
        fw_copy(which).start()

    h_copy.wait()
    pl.semaphore_wait(barrier, len(dp_steps) + 4 + NJ - 1)
    for i in range(7):
        to_dp(pm, pm_s, pm_r, i).start()
    for item in far[0]:
        hx_copy(*item).start()
    own_copy.start()
    for n, (at, size) in enumerate(FWD):
        w_copies[n].wait()
        if n + 2 < NF:
            w_copies[n + 2].start()
        lg = lax.dot_general(
            hv[...].reshape(2 * L, D),
            wv[at : at + size, :],
            (((1,), (1,)), ((), ())),
            preferred_element_type=F32,
        )
        token = lax.broadcasted_iota(jnp.int32, (L, size), 0).astype(F32)
        width = min(size, V - at)
        for s in range(2):
            spot = pm[k, s : s + 1, at : at + size]
            picked = jnp.sum(
                jnp.where(token == spot, lg[s * L : (s + 1) * L], 0.0), axis=0, keepdims=True
            )
            b = bias[:, at : at + width]
            if width < size:
                b = jnp.concatenate([b, jnp.zeros((1, size - width), F32)], axis=1)
            valid = spot < lens[s].astype(F32)
            sel[k, s : s + 1, at : at + size] = jnp.where(valid, jnp.maximum(picked + b, 0.0), 0.0)

    for i in range(7):
        to_dp(sel, sel_s, sel_r, i).start()
    for i in range(7):
        to_dp(pm, pm_s, pm_r, i).wait()
    for i in range(7):
        to_dp(sel, sel_s, sel_r, i).wait()
    for item in near:
        hx_copy(*item).start()

    for i in range(NK):
        qs[i : i + 1, :] = sel[i, 0:1, :]
        ps[i : i + 1, :] = sel[i, 1:2, :]
    q = jnp.log1p(qs[...])
    p = jnp.log1p(ps[...])
    first = jnp.concatenate([pm[i, 2:3, 0:128] for i in range(NK)], axis=0)
    second = jnp.concatenate([pm[i, 2:3, 128:256] for i in range(NK)], axis=0)
    margin = jnp.concatenate([pm[i, 2:3, 256:384] for i in range(NK)], axis=0)

    def hit(a, b):
        return jnp.where(a == b, 1.0, 0.0)

    diff = jnp.zeros((NK, VP), F32)
    for i in range(NK):
        sign = hit(first, float(i)) - hit(second, float(i))
        diff += jnp.tile(sign, (1, VP // 128)) * p[i : i + 1, :]
    dl[j] = jnp.broadcast_to(jnp.sum(q * diff, axis=1, keepdims=True), (NK, 128))

    def dl_copy(i):
        return pltpu.make_async_remote_copy(
            src_ref=dl.at[j],
            dst_ref=dl.at[j],
            send_sem=dl_s.at[i],
            recv_sem=dl_r.at[i],
            device_id={"vocab": (j + i) % NJ},
            device_id_type=MESH,
        )

    for i in range(1, NJ):
        dl_copy(i).start()

    reg = objective_factor * regularizer_coefficient * 2.0 / NK / NK
    mean_q = reg * jnp.sum(q, axis=0, keepdims=True)
    mean_p = reg * jnp.sum(p, axis=0, keepdims=True)
    inv_q = jnp.where(qs[...] > 0.0, 1.0 / (1.0 + qs[...]), 0.0)
    inv_p = jnp.where(ps[...] > 0.0, 1.0 / (1.0 + ps[...]), 0.0)

    for i in range(1, NJ):
        dl_copy(i).wait()
    delta = dl[0]
    for i in range(1, NJ):
        delta += dl[i]
    delta = delta / logit_divisor
    weight_of = (objective_factor * 2.0 / NK / logit_divisor) * (delta - margin)
    ds[0] = (jnp.tile(weight_of, (1, VP // 128)) * diff + mean_q) * inv_q
    row = lax.broadcasted_iota(jnp.int32, (NK, 128), 0).astype(F32)
    dp = jnp.zeros((NK, VP), F32)
    for i in range(NK):
        sign = hit(first[i : i + 1, :], row) - hit(second[i : i + 1, :], row)
        dp += jnp.tile(sign * weight_of[i : i + 1, :], (1, VP // 128)) * q[i : i + 1, :]
    ds[1] = (dp + mean_p) * inv_p

    token16 = lax.broadcasted_iota(jnp.int32, (16, VP), 0).astype(F32)
    own_d = [ds[s, pl.ds(k, 1), :].astype(BF) for s in range(2)]
    own_p = [pm[k, s : s + 1, :].astype(BF) for s in range(2)]
    for crel in range(2):
        for yrel in range(4):
            for zrel in range(2):
                base = (vid(zrel, yrel, crel) * 16).astype(F32)
                token = (token16 + base).astype(BF)
                for s in range(2):
                    r = crel * 256 + yrel * 64 + zrel * 32 + s * 16
                    g[r : r + 16, :] = jnp.where(token == own_p[s], own_d[s], jnp.zeros((), BF))

    def height(c):
        return 32 if c in ZFIRST else 64

    def sib_copy(c):
        return pltpu.make_async_remote_copy(
            src_ref=sibs.at[c],
            dst_ref=sibr.at[c],
            send_sem=sib_s.at[c],
            recv_sem=sib_r.at[c],
            device_id={"vocab": sibling},
            device_id_type=MESH,
        )

    def y_copy(c, which):
        n = height(c)
        side = TURN[c]
        src = st.at[c, pl.ds((128, BACK[side], FORTH[side])[which], n)]
        if which == 0:
            dst = r1.at[c, 0:n]
        else:
            dst = r2.at[c, which - 1, 0:n]
        return pltpu.make_async_remote_copy(
            src_ref=src,
            dst_ref=dst,
            send_sem=y_s.at[c, which],
            recv_sem=y_r.at[c, which],
            device_id={"vocab": (up, down)[side if which != 1 else 1 - side]},
            device_id_type=MESH,
        )

    def z_copy(c):
        n = 128 if c in ZFIRST else 32
        return pltpu.make_async_remote_copy(
            src_ref=zst.at[c, 0:n],
            dst_ref=r3.at[c, 0:n],
            send_sem=z_s.at[c],
            recv_sem=z_r.at[c],
            device_id={"vocab": across},
            device_id_type=MESH,
        )

    def pair_sum(c, at, n):
        return ownf[c, at : at + n] + sibr[c, at : at + n].astype(F32)

    def put(c, total):
        gh_out[0, :, c * HC : (c + 1) * HC] = total[0:16].astype(BF)
        gh_out[1, :, c * HC : (c + 1) * HC] = total[16:32].astype(BF)

    def y_first(c, stage):
        forth, back = FORTH[TURN[c]], BACK[TURN[c]]
        if stage == 1:
            sib_copy(c).wait_recv()
            st[c, 128:192] = pair_sum(c, 128, 64).astype(BF)
            y_copy(c, 0).start()
            st[c, back : back + 64] = pair_sum(c, back, 64).astype(BF)
            y_copy(c, 1).start()
        elif stage == 2:
            y_copy(c, 0).wait_recv()
            st[c, forth : forth + 64] = (pair_sum(c, forth, 64) + r1[c].astype(F32)).astype(BF)
            y_copy(c, 2).start()
        elif stage == 3:
            y_copy(c, 1).wait_recv()
            y_copy(c, 2).wait_recv()
            total = pair_sum(c, 0, 64) + r2[c, 0].astype(F32) + r2[c, 1].astype(F32)
            zst[c, 0:32] = total[32:64].astype(BF)
            z_copy(c).start()
            ownf[c, 0:32] = total[0:32]
        else:
            z_copy(c).wait_recv()
            put(c, ownf[c, 0:32] + r3[c, 0:32].astype(F32))

    def z_first(c, stage):
        forth, back = FORTH[TURN[c]], BACK[TURN[c]]
        if stage == 1:
            sib_copy(c).wait_recv()
            for i in range(4):
                zst[c, 32 * i : 32 * i + 32] = pair_sum(c, 64 * i + 32, 32).astype(BF)
            z_copy(c).start()
        elif stage == 2:
            z_copy(c).wait_recv()

            def total(at):
                return pair_sum(c, at, 32) + r3[c, at // 2 : at // 2 + 32].astype(F32)

            st[c, 128:160] = total(128).astype(BF)
            y_copy(c, 0).start()
            st[c, back : back + 32] = total(back).astype(BF)
            y_copy(c, 1).start()
            ownf[c, forth : forth + 32] = total(forth)
            ownf[c, 0:32] = total(0)
        elif stage == 3:
            y_copy(c, 0).wait_recv()
            st[c, forth : forth + 32] = (
                ownf[c, forth : forth + 32] + r1[c, 0:32].astype(F32)
            ).astype(BF)
            y_copy(c, 2).start()
        else:
            y_copy(c, 1).wait_recv()
            y_copy(c, 2).wait_recv()
            put(c, ownf[c, 0:32] + r2[c, 0, 0:32].astype(F32) + r2[c, 1, 0:32].astype(F32))

    def at_point(t):
        for c, stage in PLAN.get(t, ()):
            if c in ZFIRST:
                z_first(c, stage)
            else:
                y_first(c, stage)
        if t == 0:
            for item in far[1]:
                hx_copy(*item).start()
        if t == 3:
            pass_on(1)
        if t == 6:
            pass_on(0)
        if t == 9:
            pass_on(2)

    for c in range(NH):
        part = jnp.dot(g[...], wv[:, c * HC : (c + 1) * HC], preferred_element_type=F32)
        sibs[c] = part[256:512].astype(BF)
        sib_copy(c).start()
        ownf[c] = part[0:256]
        at_point(c)

    token256 = lax.broadcasted_iota(jnp.int32, (L, WC), 0).astype(F32).astype(BF)

    for dz in range(2):
        base = ((zl + dz) % 2) * 4
        if dz == 0:
            fw_copy(0).wait_recv()
        else:
            fw_copy(1).wait_recv()
            fw_copy(2).wait_recv()
        for n in range(NW):
            cols = slice(n * WC, (n + 1) * WC)
            for i in range(4):
                for s in range(2):
                    spot = pm[base + i, s : s + 1, cols].astype(BF)
                    val = ds[s, pl.ds(base + i, 1), cols].astype(BF)
                    r = (i * 2 + s) * L
                    gc[r : r + L, :] = jnp.where(token256 == spot, val, jnp.zeros((), BF))
            out = lax.dot_general(
                gc[...],
                hx[pl.ds(base, 4)].reshape(4 * 2 * L, DB),
                (((0,), (0,)), ((), ())),
                preferred_element_type=F32,
            )
            rows = slice(n * WC, min((n + 1) * WC, V))
            out = out[0 : rows.stop - rows.start]
            if dz == 0:
                gw_out[rows, :] = out
            else:
                gw_out[rows, :] += out
            at_point(NH + dz * NW + n)

    for t in range(NH + 2 * NW, NH + 2 * NW + 4):
        at_point(t)

    for item in near + far[0] + far[1]:
        hx_copy(*item).wait_send()
    for which in range(3):
        fw_copy(which).wait_send()
    for c in range(NH):
        sib_copy(c).wait_send()
        for which in range(3):
            y_copy(c, which).wait_send()
        z_copy(c).wait_send()


def local(hidden, weight, bias, positions, lengths, pairs, margins):
    vmem = pl.BlockSpec(memory_space=pltpu.VMEM)
    smem = pl.BlockSpec(memory_space=pltpu.SMEM)
    hbm = pl.BlockSpec(memory_space=pl.ANY)
    dma = pltpu.SemaphoreType.DMA
    scratch = [
        pltpu.VMEM((VP, D), BF),
        pltpu.VMEM((2, 2, 2, L // 4, D), BF),
        pltpu.VMEM((NK, 2, 2, 2, L // 4, DB), BF),
        pltpu.VMEM((2 * L, VP), BF),
        pltpu.VMEM((NK * L, WC), BF),
        pltpu.VMEM((NH, 256, HC), BF),
        pltpu.VMEM((NH, 256, HC), BF),
        pltpu.VMEM((NH, 256, HC), F32),
        pltpu.VMEM((NH, 256, HC), BF),
        pltpu.VMEM((NH, 64, HC), BF),
        pltpu.VMEM((NH, 2, 64, HC), BF),
        pltpu.VMEM((NH, 128, HC), BF),
        pltpu.VMEM((NH, 128, HC), BF),
        pltpu.VMEM((NK, 4, VP), F32),
        pltpu.VMEM((NK, 2, VP), F32),
        pltpu.VMEM((NJ, NK, 128), F32),
        pltpu.VMEM((NK, VP), F32),
        pltpu.VMEM((NK, VP), F32),
        pltpu.VMEM((2, NK, VP), F32),
        dma((NF,)),
        dma,
        dma,
        dma((7,)),
        dma((7,)),
        dma((7, 2, 2)),
        dma((7, 2, 2)),
        dma((3,)),
        dma((3,)),
        dma((7,)),
        dma((7,)),
        dma((NJ,)),
        dma((NJ,)),
        dma((NH,)),
        dma((NH,)),
        dma((NH, 3)),
        dma((NH, 3)),
        dma((NH,)),
        dma((NH,)),
    ]
    gh, gw = pl.pallas_call(
        kernel,
        out_shape=(
            pltpu.VMEM((2, 16, D), BF),
            pltpu.VMEM((V, DB), F32),
        ),
        in_specs=[hbm, hbm, vmem, vmem, smem, smem, smem],
        out_specs=(vmem, vmem),
        scratch_shapes=scratch,
        compiler_params=pltpu.CompilerParams(
            collective_id=0, has_side_effects=True, vmem_limit_bytes=56 * 2**20
        ),
        cost_estimate=pl.CostEstimate(
            flops=6 * 512 * V * D, bytes_accessed=24 * 2**20, transcendentals=0
        ),
        name="splade_backward",
    )(
        hidden.reshape(2, 2, 2, L // 4, D),
        weight,
        bias.reshape(1, V),
        positions,
        lengths.reshape(2),
        pairs.reshape(2),
        margins,
    )
    return gh.reshape(2, 1, 16, D), gw


def solution(mesh):
    in_specs = (
        P(None, "dp", None, None),
        P("vocab", None),
        P("vocab"),
        P(None, "dp", "vocab"),
        P(None, "dp"),
        P("dp", None),
        P("dp"),
    )
    out_specs = (P(None, "dp", "vocab", None), P("vocab", "dp"))
    return jax.shard_map(local, mesh=mesh, in_specs=in_specs, out_specs=out_specs, check_vma=False)
```

```python
import jax
import jax.numpy as jnp
from jax import lax
from jax.experimental import pallas as pl
from jax.experimental.pallas import tpu as pltpu
from jax.sharding import PartitionSpec as P

logit_divisor = 16.0
objective_factor = 256.0
regularizer_coefficient = 0.1

BF = jnp.bfloat16
F32 = jnp.float32
MESH = pl.DeviceIdType.MESH

V = 2000
VP = 2048
D = 4096
L = 256
NK = 8
NJ = 16
DB = 512
FWD = ((0, 256), (256, 256), (512, 512), (1024, 1024))
NF = len(FWD)
HC = 512
NH = D // HC
WC = 512
NW = VP // WC
ZFIRST = (0, 4, 7)
TURN = (0, 1, 0, 1, 1, 1, 0, 0)
FORTH, BACK = (64, 192), (192, 64)
PLAN = {
    2: ((0, 1),),
    3: ((1, 1),),
    4: ((2, 1),),
    5: ((3, 1),),
    6: ((1, 2), (4, 1), (5, 1)),
    7: ((0, 2), (2, 2)),
    8: ((3, 2), (1, 3), (6, 1), (7, 1)),
    9: ((0, 3), (5, 2)),
    10: ((2, 3), (4, 2), (3, 3), (1, 4)),
    11: ((0, 4), (6, 2)),
    12: ((5, 3), (7, 2)),
    13: ((2, 4), (3, 4), (4, 3)),
    14: ((6, 3), (7, 3)),
    15: ((4, 4), (5, 4), (7, 4), (6, 4)),
}


def kernel(
    h_hbm,
    w_hbm,
    bias,
    pos_in,
    lens,
    pairs,
    margins,
    gh_out,
    gw_out,
    wv,
    hv,
    hx,
    g,
    gc,
    sibs,
    sibr,
    ownf,
    st,
    r1,
    r2,
    zst,
    r3,
    pm,
    sel,
    dl,
    qs,
    ps,
    ds,
    w_sem,
    h_sem,
    own_sem,
    pm_s,
    pm_r,
    hx_s,
    hx_r,
    fw_s,
    fw_r,
    sel_s,
    sel_r,
    dl_s,
    dl_r,
    sib_s,
    sib_r,
    y_s,
    y_r,
    z_s,
    z_r,
):
    k = lax.axis_index("dp")
    j = lax.axis_index("vocab")
    core = j % 2
    y = (j // 2) % 4
    zh = j // 8
    zl = k // 4
    x = k % 4

    def vid(zrel, yrel, crel):
        return ((zh + zrel) % 2) * 8 + ((y + yrel) % 4) * 2 + (core + crel) % 2

    def kid(dz, dx):
        return ((zl + dz) % 2) * 4 + (x + dx) % 4

    sibling = vid(0, 0, 1)
    up = vid(0, 1, 0)
    down = vid(0, 3, 0)
    across = vid(1, 0, 0)
    dp_steps = [(dz, dx) for dz in range(2) for dx in range(4) if (dz, dx) != (0, 0)]

    halves = (slice(0, D // 2), slice(D // 2, D))
    h_copies = [
        pltpu.make_async_copy(h_hbm.at[..., cols], hv.at[..., cols], h_sem.at[i])
        for i, cols in enumerate(halves)
    ]
    w0_copies = [
        pltpu.make_async_copy(
            w_hbm.at[0 : FWD[0][1], cols], wv.at[0 : FWD[0][1], cols], w_sem.at[(0, NF)[i]]
        )
        for i, cols in enumerate(halves)
    ]
    w_copies = [None]
    for n, (at, size) in enumerate(FWD):
        if n > 0:
            rows = min(size, V - at)
            c = pltpu.make_async_copy(
                w_hbm.at[pl.ds(at, rows), :], wv.at[pl.ds(at, rows), :], w_sem.at[n]
            )
            w_copies.append(c)
    h_copies[0].start()
    w0_copies[0].start()

    barrier = pltpu.get_barrier_semaphore()
    for dz, dx in dp_steps:
        pl.semaphore_signal(barrier, inc=1, device_id={"dp": kid(dz, dx)}, device_id_type=MESH)
    for dx in range(1, 4):
        pl.semaphore_signal(
            barrier,
            inc=1,
            device_id={"dp": kid(1, dx), "vocab": across},
            device_id_type=MESH,
        )
    for i in range(1, NJ):
        zr, yr, cr = i // 8, (i // 2) % 4, i % 2
        pl.semaphore_signal(
            barrier,
            inc=1,
            device_id={"dp": kid(zr, 0), "vocab": vid(zr, yr, cr)},
            device_id_type=MESH,
        )
    pl.semaphore_signal(barrier, inc=1, device_id={"vocab": across}, device_id_type=MESH)

    h_copies[1].start()
    w0_copies[1].start()
    own_copy = pltpu.make_async_copy(
        hv.at[core, :, :, :, pl.ds(pl.multiple_of(k * DB, DB), DB)],
        hx.at[k, core],
        own_sem,
    )
    wv[V:VP, :] = jnp.zeros((VP - V, D), BF)

    pad = jnp.zeros((1, VP - V), F32)
    for s in range(2):
        pm[k, s : s + 1, :] = jnp.concatenate([pos_in[s].astype(F32), pad], axis=1)
    pm[k, 2:3, 0:128] = jnp.full((1, 128), pairs[0], jnp.int32).astype(F32)
    pm[k, 2:3, 128:256] = jnp.full((1, 128), pairs[1], jnp.int32).astype(F32)
    pm[k, 2:3, 256:384] = jnp.full((1, 128), margins[0], F32)
    pm[k, 2:3, 384:VP] = jnp.zeros((1, VP - 384), F32)
    pm[k, 3:4, :] = jnp.zeros((1, VP), F32)

    def to_dp(ref, ssem, rsem, i):
        dz, dx = dp_steps[i]
        return pltpu.make_async_remote_copy(
            src_ref=ref.at[k],
            dst_ref=ref.at[k],
            send_sem=ssem.at[i],
            recv_sem=rsem.at[i],
            device_id={"dp": kid(dz, dx)},
            device_id_type=MESH,
        )

    near = [(i, None, None) for i in range(7) if dp_steps[i][0] == 0]
    far = [
        [(i, part, sub) for i in range(7) if dp_steps[i][0] == 1 for part in range(2)]
        for sub in range(2)
    ]

    def hx_copy(i, part, sub):
        dz, dx = dp_steps[i]
        other = kid(dz, dx)
        cols = pl.ds(pl.multiple_of(other * DB, DB), DB)
        if part is None:
            src, dst, sems = hv.at[core, :, :, :, cols], hx.at[k, core], (i, 0, 0)
            to = {"dp": other}
        else:
            src, dst = hv.at[core, part, sub, :, cols], hx.at[k, core, part, sub]
            sems, to = (i, part, sub), {"dp": other, "vocab": vid(part, 0, 0)}
        return pltpu.make_async_remote_copy(
            src_ref=src,
            dst_ref=dst,
            send_sem=hx_s.at[sems],
            recv_sem=hx_r.at[sems],
            device_id=to,
            device_id_type=MESH,
        )

    def fw_copy(which):
        if which == 0:
            ref = hx.at[pl.ds(zl * 4, 4), core]
        else:
            ref = hx.at[pl.ds((1 - zl) * 4, 4), core, :, which - 1]
        return pltpu.make_async_remote_copy(
            src_ref=ref,
            dst_ref=ref,
            send_sem=fw_s.at[which],
            recv_sem=fw_r.at[which],
            device_id={"vocab": sibling},
            device_id_type=MESH,
        )

    def pass_on(which):
        if which == 0:
            own_copy.wait()
            batch = near
        else:
            batch = far[which - 1]
        for item in batch:
            hx_copy(*item).wait_recv()
        fw_copy(which).start()

    def logits(rows, cols):
        return lax.dot_general(
            hv[..., cols].reshape(2 * L, cols.stop - cols.start),
            wv[rows, cols],
            (((1,), (1,)), ((), ())),
            preferred_element_type=F32,
        )

    pl.semaphore_wait(barrier, len(dp_steps) + 3 + NJ)
    for i in range(7):
        to_dp(pm, pm_s, pm_r, i).start()
    for n, (at, size) in enumerate(FWD):
        rows = slice(at, at + size)
        if n == 0:
            h_copies[0].wait()
            w0_copies[0].wait()
            w_copies[1].start()
            lg = logits(rows, halves[0])
            h_copies[1].wait()
            w0_copies[1].wait()
            for item in far[0]:
                hx_copy(*item).start()
            own_copy.start()
            w_copies[2].start()
            lg += logits(rows, halves[1])
        else:
            w_copies[n].wait()
            if 2 < n + 2 < NF:
                w_copies[n + 2].start()
            lg = logits(rows, slice(0, D))
        token = lax.broadcasted_iota(jnp.int32, (L, size), 0).astype(F32)
        width = min(size, V - at)
        for s in range(2):
            spot = pm[k, s : s + 1, at : at + size]
            picked = jnp.sum(
                jnp.where(token == spot, lg[s * L : (s + 1) * L], 0.0), axis=0, keepdims=True
            )
            b = bias[:, at : at + width]
            if width < size:
                b = jnp.concatenate([b, jnp.zeros((1, size - width), F32)], axis=1)
            valid = spot < lens[s].astype(F32)
            sel[k, s : s + 1, at : at + size] = jnp.where(valid, jnp.maximum(picked + b, 0.0), 0.0)

    for i in range(7):
        to_dp(sel, sel_s, sel_r, i).start()
    for i in range(7):
        to_dp(pm, pm_s, pm_r, i).wait_recv()
    first = jnp.concatenate([pm[i, 2:3, 0:128] for i in range(NK)], axis=0)
    second = jnp.concatenate([pm[i, 2:3, 128:256] for i in range(NK)], axis=0)
    margin = jnp.concatenate([pm[i, 2:3, 256:384] for i in range(NK)], axis=0)

    for i in range(7):
        to_dp(sel, sel_s, sel_r, i).wait_recv()
    for i in range(NK):
        qs[i : i + 1, :] = sel[i, 0:1, :]
        ps[i : i + 1, :] = sel[i, 1:2, :]
    q = jnp.log1p(qs[...])
    p = jnp.log1p(ps[...])
    def hit(a, b):
        return jnp.where(a == b, 1.0, 0.0)

    diff = jnp.zeros((NK, VP), F32)
    for i in range(NK):
        sign = hit(first, float(i)) - hit(second, float(i))
        diff += jnp.tile(sign, (1, VP // 128)) * p[i : i + 1, :]
    dl[j] = jnp.broadcast_to(jnp.sum(q * diff, axis=1, keepdims=True), (NK, 128))

    def dl_copy(i):
        zr, yr, cr = i // 8, (i // 2) % 4, i % 2
        return pltpu.make_async_remote_copy(
            src_ref=dl.at[j],
            dst_ref=dl.at[j],
            send_sem=dl_s.at[i],
            recv_sem=dl_r.at[i],
            device_id={"dp": kid(zr, 0), "vocab": vid(zr, yr, cr)},
            device_id_type=MESH,
        )

    for i in range(1, NJ):
        dl_copy(i).start()
    for item in near:
        hx_copy(*item).start()

    reg = objective_factor * regularizer_coefficient * 2.0 / NK / NK
    mean_q = reg * jnp.sum(q, axis=0, keepdims=True)
    mean_p = reg * jnp.sum(p, axis=0, keepdims=True)
    inv_q = jnp.where(qs[...] > 0.0, 1.0 / (1.0 + qs[...]), 0.0)
    inv_p = jnp.where(ps[...] > 0.0, 1.0 / (1.0 + ps[...]), 0.0)

    for i in range(1, NJ):
        dl_copy(i).wait_recv()
    delta = dl[0]
    for i in range(1, NJ):
        delta += dl[i]
    delta = delta / logit_divisor
    weight_of = (objective_factor * 2.0 / NK / logit_divisor) * (delta - margin)
    ds[0] = (jnp.tile(weight_of, (1, VP // 128)) * diff + mean_q) * inv_q
    row = lax.broadcasted_iota(jnp.int32, (NK, 128), 0).astype(F32)
    dp = jnp.zeros((NK, VP), F32)
    for i in range(NK):
        sign = hit(first[i : i + 1, :], row) - hit(second[i : i + 1, :], row)
        dp += jnp.tile(sign * weight_of[i : i + 1, :], (1, VP // 128)) * q[i : i + 1, :]
    ds[1] = (dp + mean_p) * inv_p

    token16 = lax.broadcasted_iota(jnp.int32, (16, VP), 0).astype(F32)
    own_d = [ds[s, pl.ds(k, 1), :].astype(BF) for s in range(2)]
    own_p = [pm[k, s : s + 1, :].astype(BF) for s in range(2)]
    for crel in range(2):
        for yrel in range(4):
            for zrel in range(2):
                base = (vid(zrel, yrel, crel) * 16).astype(F32)
                token = (token16 + base).astype(BF)
                for s in range(2):
                    r = crel * 256 + yrel * 64 + zrel * 32 + s * 16
                    g[r : r + 16, :] = jnp.where(token == own_p[s], own_d[s], jnp.zeros((), BF))

    def height(c):
        return 32 if c in ZFIRST else 64

    def sib_copy(c):
        return pltpu.make_async_remote_copy(
            src_ref=sibs.at[c],
            dst_ref=sibr.at[c],
            send_sem=sib_s.at[c],
            recv_sem=sib_r.at[c],
            device_id={"vocab": sibling},
            device_id_type=MESH,
        )

    def y_copy(c, which):
        n = height(c)
        side = TURN[c]
        src = st.at[c, pl.ds((128, BACK[side], FORTH[side])[which], n)]
        if which == 0:
            dst = r1.at[c, 0:n]
        else:
            dst = r2.at[c, which - 1, 0:n]
        return pltpu.make_async_remote_copy(
            src_ref=src,
            dst_ref=dst,
            send_sem=y_s.at[c, which],
            recv_sem=y_r.at[c, which],
            device_id={"vocab": (up, down)[side if which != 1 else 1 - side]},
            device_id_type=MESH,
        )

    def z_copy(c):
        n = 128 if c in ZFIRST else 32
        return pltpu.make_async_remote_copy(
            src_ref=zst.at[c, 0:n],
            dst_ref=r3.at[c, 0:n],
            send_sem=z_s.at[c],
            recv_sem=z_r.at[c],
            device_id={"vocab": across},
            device_id_type=MESH,
        )

    def pair_sum(c, at, n):
        return ownf[c, at : at + n] + sibr[c, at : at + n].astype(F32)

    def put(c, total):
        gh_out[0, :, c * HC : (c + 1) * HC] = total[0:16].astype(BF)
        gh_out[1, :, c * HC : (c + 1) * HC] = total[16:32].astype(BF)

    def y_first(c, stage):
        forth, back = FORTH[TURN[c]], BACK[TURN[c]]
        if stage == 1:
            sib_copy(c).wait_recv()
            st[c, 128:192] = pair_sum(c, 128, 64).astype(BF)
            y_copy(c, 0).start()
            st[c, back : back + 64] = pair_sum(c, back, 64).astype(BF)
            y_copy(c, 1).start()
        elif stage == 2:
            y_copy(c, 0).wait_recv()
            st[c, forth : forth + 64] = (pair_sum(c, forth, 64) + r1[c].astype(F32)).astype(BF)
            y_copy(c, 2).start()
        elif stage == 3:
            y_copy(c, 1).wait_recv()
            y_copy(c, 2).wait_recv()
            total = pair_sum(c, 0, 64) + r2[c, 0].astype(F32) + r2[c, 1].astype(F32)
            zst[c, 0:32] = total[32:64].astype(BF)
            z_copy(c).start()
            ownf[c, 0:32] = total[0:32]
        else:
            z_copy(c).wait_recv()
            put(c, ownf[c, 0:32] + r3[c, 0:32].astype(F32))

    def z_first(c, stage):
        forth, back = FORTH[TURN[c]], BACK[TURN[c]]
        if stage == 1:
            sib_copy(c).wait_recv()
            for i in range(4):
                zst[c, 32 * i : 32 * i + 32] = pair_sum(c, 64 * i + 32, 32).astype(BF)
            z_copy(c).start()
        elif stage == 2:
            z_copy(c).wait_recv()

            def total(at):
                return pair_sum(c, at, 32) + r3[c, at // 2 : at // 2 + 32].astype(F32)

            st[c, 128:160] = total(128).astype(BF)
            y_copy(c, 0).start()
            st[c, back : back + 32] = total(back).astype(BF)
            y_copy(c, 1).start()
            ownf[c, forth : forth + 32] = total(forth)
            ownf[c, 0:32] = total(0)
        elif stage == 3:
            y_copy(c, 0).wait_recv()
            st[c, forth : forth + 32] = (
                ownf[c, forth : forth + 32] + r1[c, 0:32].astype(F32)
            ).astype(BF)
            y_copy(c, 2).start()
        else:
            y_copy(c, 1).wait_recv()
            y_copy(c, 2).wait_recv()
            put(c, ownf[c, 0:32] + r2[c, 0, 0:32].astype(F32) + r2[c, 1, 0:32].astype(F32))

    def at_point(t):
        for c, stage in PLAN.get(t, ()):
            if c in ZFIRST:
                z_first(c, stage)
            else:
                y_first(c, stage)
        if t == 0:
            for item in far[1]:
                hx_copy(*item).start()
        if t == 3:
            pass_on(1)
        if t == 6:
            pass_on(0)
        if t == 9:
            pass_on(2)

    for c in range(NH):
        part = jnp.dot(g[...], wv[:, c * HC : (c + 1) * HC], preferred_element_type=F32)
        sibs[c] = part[256:512].astype(BF)
        sib_copy(c).start()
        ownf[c] = part[0:256]
        at_point(c)

    token256 = lax.broadcasted_iota(jnp.int32, (L, WC), 0).astype(F32).astype(BF)

    for dz in range(2):
        base = ((zl + dz) % 2) * 4
        if dz == 0:
            fw_copy(0).wait_recv()
        else:
            fw_copy(1).wait_recv()
            fw_copy(2).wait_recv()
        for n in range(NW):
            cols = slice(n * WC, (n + 1) * WC)
            for i in range(4):
                for s in range(2):
                    spot = pm[base + i, s : s + 1, cols].astype(BF)
                    val = ds[s, pl.ds(base + i, 1), cols].astype(BF)
                    r = (i * 2 + s) * L
                    gc[r : r + L, :] = jnp.where(token256 == spot, val, jnp.zeros((), BF))
            out = lax.dot_general(
                gc[...],
                hx[pl.ds(base, 4)].reshape(4 * 2 * L, DB),
                (((0,), (0,)), ((), ())),
                preferred_element_type=F32,
            )
            rows = slice(n * WC, min((n + 1) * WC, V))
            out = out[0 : rows.stop - rows.start]
            if dz == 0:
                gw_out[rows, :] = out
            else:
                gw_out[rows, :] += out
            at_point(NH + dz * NW + n)

    for t in range(NH + 2 * NW, NH + 2 * NW + 4):
        at_point(t)

    for i in range(7):
        to_dp(pm, pm_s, pm_r, i).wait_send()
        to_dp(sel, sel_s, sel_r, i).wait_send()
    for i in range(1, NJ):
        dl_copy(i).wait_send()
    for item in near + far[0] + far[1]:
        hx_copy(*item).wait_send()
    for which in range(3):
        fw_copy(which).wait_send()
    for c in range(NH):
        sib_copy(c).wait_send()
        for which in range(3):
            y_copy(c, which).wait_send()
        z_copy(c).wait_send()


def local(hidden, weight, bias, positions, lengths, pairs, margins):
    vmem = pl.BlockSpec(memory_space=pltpu.VMEM)
    smem = pl.BlockSpec(memory_space=pltpu.SMEM)
    hbm = pl.BlockSpec(memory_space=pl.ANY)
    dma = pltpu.SemaphoreType.DMA
    scratch = [
        pltpu.VMEM((VP, D), BF),
        pltpu.VMEM((2, 2, 2, L // 4, D), BF),
        pltpu.VMEM((NK, 2, 2, 2, L // 4, DB), BF),
        pltpu.VMEM((2 * L, VP), BF),
        pltpu.VMEM((NK * L, WC), BF),
        pltpu.VMEM((NH, 256, HC), BF),
        pltpu.VMEM((NH, 256, HC), BF),
        pltpu.VMEM((NH, 256, HC), F32),
        pltpu.VMEM((NH, 256, HC), BF),
        pltpu.VMEM((NH, 64, HC), BF),
        pltpu.VMEM((NH, 2, 64, HC), BF),
        pltpu.VMEM((NH, 128, HC), BF),
        pltpu.VMEM((NH, 128, HC), BF),
        pltpu.VMEM((NK, 4, VP), F32),
        pltpu.VMEM((NK, 2, VP), F32),
        pltpu.VMEM((NJ, NK, 128), F32),
        pltpu.VMEM((NK, VP), F32),
        pltpu.VMEM((NK, VP), F32),
        pltpu.VMEM((2, NK, VP), F32),
        dma((NF + 1,)),
        dma((2,)),
        dma,
        dma((7,)),
        dma((7,)),
        dma((7, 2, 2)),
        dma((7, 2, 2)),
        dma((3,)),
        dma((3,)),
        dma((7,)),
        dma((7,)),
        dma((NJ,)),
        dma((NJ,)),
        dma((NH,)),
        dma((NH,)),
        dma((NH, 3)),
        dma((NH, 3)),
        dma((NH,)),
        dma((NH,)),
    ]
    gh, gw = pl.pallas_call(
        kernel,
        out_shape=(
            pltpu.VMEM((2, 16, D), BF),
            pltpu.VMEM((V, DB), F32),
        ),
        in_specs=[hbm, hbm, vmem, vmem, smem, smem, smem],
        out_specs=(vmem, vmem),
        scratch_shapes=scratch,
        compiler_params=pltpu.CompilerParams(
            collective_id=0, has_side_effects=True, vmem_limit_bytes=56 * 2**20
        ),
        cost_estimate=pl.CostEstimate(
            flops=6 * 512 * V * D, bytes_accessed=24 * 2**20, transcendentals=0
        ),
        name="splade_backward",
    )(
        hidden.reshape(2, 2, 2, L // 4, D),
        weight,
        bias.reshape(1, V),
        positions,
        lengths.reshape(2),
        pairs.reshape(2),
        margins,
    )
    return gh.reshape(2, 1, 16, D), gw


def solution(mesh):
    in_specs = (
        P(None, "dp", None, None),
        P("vocab", None),
        P("vocab"),
        P(None, "dp", "vocab"),
        P(None, "dp"),
        P("dp", None),
        P("dp"),
    )
    out_specs = (P(None, "dp", "vocab", None), P("vocab", "dp"))
    return jax.shard_map(local, mesh=mesh, in_specs=in_specs, out_specs=out_specs, check_vma=False)
```

```python
import jax
import jax.numpy as jnp
from jax import lax
from jax.experimental import pallas as pl
from jax.experimental.pallas import tpu as pltpu
from jax.sharding import PartitionSpec as P

logit_divisor = 16.0
objective_factor = 256.0
regularizer_coefficient = 0.1

BF = jnp.bfloat16
F32 = jnp.float32
MESH = pl.DeviceIdType.MESH

V = 2000
VP = 2048
D = 4096
L = 256
NK = 8
NJ = 16
DB = 512
FWD = ((0, 256), (256, 256), (512, 512), (1024, 1024))
NF = len(FWD)
HC = 512
NH = D // HC
WC = 512
NW = VP // WC
ZFIRST = (0, 4, 7)
TURN = (0, 1, 0, 1, 1, 1, 0, 0)
FORTH, BACK = (64, 192), (192, 64)
PLAN = {
    2: ((0, 1),),
    3: ((1, 1),),
    4: ((2, 1),),
    5: ((3, 1),),
    6: ((1, 2), (4, 1), (5, 1)),
    7: ((0, 2), (2, 2)),
    8: ((3, 2), (1, 3), (6, 1), (7, 1)),
    9: ((0, 3), (5, 2)),
    10: ((2, 3), (4, 2), (3, 3), (1, 4)),
    11: ((0, 4), (6, 2)),
    12: ((5, 3), (7, 2)),
    13: ((2, 4), (3, 4), (4, 3)),
    14: ((6, 3), (7, 3)),
    15: ((4, 4), (5, 4), (7, 4), (6, 4)),
}


def kernel(
    h_hbm,
    w_hbm,
    bias,
    pos_in,
    lens,
    pairs,
    margins,
    gh_out,
    gw_out,
    wv,
    hv,
    hx,
    g,
    gc,
    sibs,
    sibr,
    ownf,
    st,
    r1,
    r2,
    zst,
    r3,
    pm,
    sel,
    dl,
    qs,
    ps,
    ds,
    w_sem,
    h_sem,
    own_sem,
    pm_s,
    pm_r,
    hx_s,
    hx_r,
    fw_s,
    fw_r,
    sel_s,
    sel_r,
    dl_s,
    dl_r,
    sib_s,
    sib_r,
    y_s,
    y_r,
    z_s,
    z_r,
):
    k = lax.axis_index("dp")
    j = lax.axis_index("vocab")
    core = j % 2
    y = (j // 2) % 4
    zh = j // 8
    zl = k // 4
    x = k % 4

    def vid(zrel, yrel, crel):
        return ((zh + zrel) % 2) * 8 + ((y + yrel) % 4) * 2 + (core + crel) % 2

    def kid(dz, dx):
        return ((zl + dz) % 2) * 4 + (x + dx) % 4

    sibling = vid(0, 0, 1)
    up = vid(0, 1, 0)
    down = vid(0, 3, 0)
    across = vid(1, 0, 0)
    dp_steps = [(dz, dx) for dz in range(2) for dx in range(4) if (dz, dx) != (0, 0)]

    halves = (slice(0, D // 2), slice(D // 2, D))
    h_copies = [
        pltpu.make_async_copy(h_hbm.at[..., cols], hv.at[..., cols], h_sem.at[i])
        for i, cols in enumerate(halves)
    ]
    w0_copies = [
        pltpu.make_async_copy(
            w_hbm.at[0 : FWD[0][1], cols], wv.at[0 : FWD[0][1], cols], w_sem.at[(0, NF)[i]]
        )
        for i, cols in enumerate(halves)
    ]
    w_copies = [None]
    for n, (at, size) in enumerate(FWD):
        if n > 0:
            rows = min(size, V - at)
            c = pltpu.make_async_copy(
                w_hbm.at[pl.ds(at, rows), :], wv.at[pl.ds(at, rows), :], w_sem.at[n]
            )
            w_copies.append(c)
    h_copies[0].start()
    w0_copies[0].start()

    barrier = pltpu.get_barrier_semaphore()
    for dz, dx in dp_steps:
        pl.semaphore_signal(barrier, inc=1, device_id={"dp": kid(dz, dx)}, device_id_type=MESH)
    for dx in range(1, 4):
        pl.semaphore_signal(
            barrier,
            inc=1,
            device_id={"dp": kid(1, dx), "vocab": across},
            device_id_type=MESH,
        )
    for i in range(1, NJ):
        zr, yr, cr = i // 8, (i // 2) % 4, i % 2
        pl.semaphore_signal(
            barrier,
            inc=1,
            device_id={"dp": kid(zr, 0), "vocab": vid(zr, yr, cr)},
            device_id_type=MESH,
        )
    pl.semaphore_signal(barrier, inc=1, device_id={"vocab": across}, device_id_type=MESH)

    h_copies[1].start()
    w0_copies[1].start()
    own_copy = pltpu.make_async_copy(
        hv.at[core, :, :, :, pl.ds(pl.multiple_of(k * DB, DB), DB)],
        hx.at[k, core],
        own_sem,
    )
    wv[V:VP, :] = jnp.zeros((VP - V, D), BF)

    pad = jnp.zeros((1, VP - V), F32)
    for s in range(2):
        pm[k, s : s + 1, :] = jnp.concatenate([pos_in[s].astype(F32), pad], axis=1)
    pm[k, 2:3, 0:128] = jnp.full((1, 128), pairs[0], jnp.int32).astype(F32)
    pm[k, 2:3, 128:256] = jnp.full((1, 128), pairs[1], jnp.int32).astype(F32)
    pm[k, 2:3, 256:384] = jnp.full((1, 128), margins[0], F32)
    pm[k, 2:3, 384:VP] = jnp.zeros((1, VP - 384), F32)
    pm[k, 3:4, :] = jnp.zeros((1, VP), F32)

    def all_of(ref, ssem, rsem):
        return pltpu.make_async_remote_copy(
            src_ref=ref,
            dst_ref=ref,
            send_sem=ssem,
            recv_sem=rsem,
            device_id={"vocab": sibling},
            device_id_type=MESH,
        )

    def to_dp(ref, ssem, rsem, i):
        dz, dx = dp_steps[i]
        return pltpu.make_async_remote_copy(
            src_ref=ref.at[k],
            dst_ref=ref.at[k],
            send_sem=ssem,
            recv_sem=rsem,
            device_id={"dp": kid(dz, dx)},
            device_id_type=MESH,
        )

    near = [(i, None, None) for i in range(7) if dp_steps[i][0] == 0]
    far = [
        [(i, part, sub) for i in range(7) if dp_steps[i][0] == 1 for part in range(2)]
        for sub in range(2)
    ]

    def hx_copy(i, part, sub):
        dz, dx = dp_steps[i]
        other = kid(dz, dx)
        cols = pl.ds(pl.multiple_of(other * DB, DB), DB)
        if part is None:
            src, dst, sems = hv.at[core, :, :, :, cols], hx.at[k, core], (i, 0, 0)
            to = {"dp": other}
        else:
            src, dst = hv.at[core, part, sub, :, cols], hx.at[k, core, part, sub]
            sems, to = (i, part, sub), {"dp": other, "vocab": vid(part, 0, 0)}
        return pltpu.make_async_remote_copy(
            src_ref=src,
            dst_ref=dst,
            send_sem=hx_s.at[0 if part is None else 1 + sub],
            recv_sem=hx_r.at[sems],
            device_id=to,
            device_id_type=MESH,
        )

    def fw_copy(which):
        if which == 0:
            ref = hx.at[pl.ds(zl * 4, 4), core]
        else:
            ref = hx.at[pl.ds((1 - zl) * 4, 4), core, :, which - 1]
        return pltpu.make_async_remote_copy(
            src_ref=ref,
            dst_ref=ref,
            send_sem=fw_s.at[which],
            recv_sem=fw_r.at[which],
            device_id={"vocab": sibling},
            device_id_type=MESH,
        )

    def pass_on(which):
        if which == 0:
            own_copy.wait()
            batch = near
        else:
            batch = far[which - 1]
        for item in batch:
            hx_copy(*item).wait_recv()
        fw_copy(which).start()

    def logits(rows, cols):
        return lax.dot_general(
            hv[..., cols].reshape(2 * L, cols.stop - cols.start),
            wv[rows, cols],
            (((1,), (1,)), ((), ())),
            preferred_element_type=F32,
        )

    pl.semaphore_wait(barrier, len(dp_steps) + 3 + NJ)
    for i in range(7):
        to_dp(pm, pm_s, pm_r, i).start()
    for n, (at, size) in enumerate(FWD):
        rows = slice(at, at + size)
        if n == 0:
            h_copies[0].wait()
            w0_copies[0].wait()
            w_copies[1].start()
            lg = logits(rows, halves[0])
            h_copies[1].wait()
            w0_copies[1].wait()
            for item in far[0]:
                hx_copy(*item).start()
            own_copy.start()
            w_copies[2].start()
            lg += logits(rows, halves[1])
        else:
            w_copies[n].wait()
            if 2 < n + 2 < NF:
                w_copies[n + 2].start()
            lg = logits(rows, slice(0, D))
        token = lax.broadcasted_iota(jnp.int32, (L, size), 0).astype(F32)
        width = min(size, V - at)
        for s in range(2):
            spot = pm[k, s : s + 1, at : at + size]
            picked = jnp.sum(
                jnp.where(token == spot, lg[s * L : (s + 1) * L], 0.0), axis=0, keepdims=True
            )
            b = bias[:, at : at + width]
            if width < size:
                b = jnp.concatenate([b, jnp.zeros((1, size - width), F32)], axis=1)
            valid = spot < lens[s].astype(F32)
            sel[k, s : s + 1, at : at + size] = jnp.where(valid, jnp.maximum(picked + b, 0.0), 0.0)

    for i in range(7):
        to_dp(sel, sel_s, sel_r, i).start()
    all_of(pm.at[0:7], pm_s, pm_r).wait_recv()
    first = jnp.concatenate([pm[i, 2:3, 0:128] for i in range(NK)], axis=0)
    second = jnp.concatenate([pm[i, 2:3, 128:256] for i in range(NK)], axis=0)
    margin = jnp.concatenate([pm[i, 2:3, 256:384] for i in range(NK)], axis=0)

    all_of(sel.at[0:7], sel_s, sel_r).wait_recv()
    for i in range(NK):
        qs[i : i + 1, :] = sel[i, 0:1, :]
        ps[i : i + 1, :] = sel[i, 1:2, :]
    q = jnp.log1p(qs[...])
    p = jnp.log1p(ps[...])
    def hit(a, b):
        return jnp.where(a == b, 1.0, 0.0)

    diff = jnp.zeros((NK, VP), F32)
    for i in range(NK):
        sign = hit(first, float(i)) - hit(second, float(i))
        diff += jnp.tile(sign, (1, VP // 128)) * p[i : i + 1, :]
    dl[j] = jnp.broadcast_to(jnp.sum(q * diff, axis=1, keepdims=True), (NK, 128))

    def dl_copy(i):
        zr, yr, cr = i // 8, (i // 2) % 4, i % 2
        return pltpu.make_async_remote_copy(
            src_ref=dl.at[j],
            dst_ref=dl.at[j],
            send_sem=dl_s,
            recv_sem=dl_r,
            device_id={"dp": kid(zr, 0), "vocab": vid(zr, yr, cr)},
            device_id_type=MESH,
        )

    for i in range(1, NJ):
        dl_copy(i).start()
    for item in near:
        hx_copy(*item).start()

    reg = objective_factor * regularizer_coefficient * 2.0 / NK / NK
    mean_q = reg * jnp.sum(q, axis=0, keepdims=True)
    mean_p = reg * jnp.sum(p, axis=0, keepdims=True)
    inv_q = jnp.where(qs[...] > 0.0, 1.0 / (1.0 + qs[...]), 0.0)
    inv_p = jnp.where(ps[...] > 0.0, 1.0 / (1.0 + ps[...]), 0.0)

    all_of(dl.at[1:NJ], dl_s, dl_r).wait_recv()
    delta = dl[0]
    for i in range(1, NJ):
        delta += dl[i]
    delta = delta / logit_divisor
    weight_of = (objective_factor * 2.0 / NK / logit_divisor) * (delta - margin)
    ds[0] = (jnp.tile(weight_of, (1, VP // 128)) * diff + mean_q) * inv_q
    row = lax.broadcasted_iota(jnp.int32, (NK, 128), 0).astype(F32)
    dp = jnp.zeros((NK, VP), F32)
    for i in range(NK):
        sign = hit(first[i : i + 1, :], row) - hit(second[i : i + 1, :], row)
        dp += jnp.tile(sign * weight_of[i : i + 1, :], (1, VP // 128)) * q[i : i + 1, :]
    ds[1] = (dp + mean_p) * inv_p

    token16 = lax.broadcasted_iota(jnp.int32, (16, VP), 0).astype(F32)
    own_d = [ds[s, pl.ds(k, 1), :].astype(BF) for s in range(2)]
    own_p = [pm[k, s : s + 1, :].astype(BF) for s in range(2)]
    for crel in range(2):
        for yrel in range(4):
            for zrel in range(2):
                base = (vid(zrel, yrel, crel) * 16).astype(F32)
                token = (token16 + base).astype(BF)
                for s in range(2):
                    r = crel * 256 + yrel * 64 + zrel * 32 + s * 16
                    g[r : r + 16, :] = jnp.where(token == own_p[s], own_d[s], jnp.zeros((), BF))

    def height(c):
        return 32 if c in ZFIRST else 64

    def sib_copy(c):
        return pltpu.make_async_remote_copy(
            src_ref=sibs.at[c],
            dst_ref=sibr.at[c],
            send_sem=sib_s,
            recv_sem=sib_r.at[c],
            device_id={"vocab": sibling},
            device_id_type=MESH,
        )

    def y_copy(c, which):
        n = height(c)
        side = TURN[c]
        src = st.at[c, pl.ds((128, BACK[side], FORTH[side])[which], n)]
        if which == 0:
            dst = r1.at[c, 0:n]
        else:
            dst = r2.at[c, which - 1, 0:n]
        return pltpu.make_async_remote_copy(
            src_ref=src,
            dst_ref=dst,
            send_sem=y_s.at[c],
            recv_sem=y_r.at[c, which],
            device_id={"vocab": (up, down)[side if which != 1 else 1 - side]},
            device_id_type=MESH,
        )

    def z_copy(c):
        n = 128 if c in ZFIRST else 32
        return pltpu.make_async_remote_copy(
            src_ref=zst.at[c, 0:n],
            dst_ref=r3.at[c, 0:n],
            send_sem=z_s.at[c],
            recv_sem=z_r.at[c],
            device_id={"vocab": across},
            device_id_type=MESH,
        )

    def pair_sum(c, at, n):
        return ownf[c, at : at + n] + sibr[c, at : at + n].astype(F32)

    def put(c, total):
        gh_out[0, :, c * HC : (c + 1) * HC] = total[0:16].astype(BF)
        gh_out[1, :, c * HC : (c + 1) * HC] = total[16:32].astype(BF)

    def y_first(c, stage):
        forth, back = FORTH[TURN[c]], BACK[TURN[c]]
        if stage == 1:
            sib_copy(c).wait_recv()
            st[c, 128:192] = pair_sum(c, 128, 64).astype(BF)
            y_copy(c, 0).start()
            st[c, back : back + 64] = pair_sum(c, back, 64).astype(BF)
            y_copy(c, 1).start()
        elif stage == 2:
            y_copy(c, 0).wait_recv()
            st[c, forth : forth + 64] = (pair_sum(c, forth, 64) + r1[c].astype(F32)).astype(BF)
            y_copy(c, 2).start()
        elif stage == 3:
            y_copy(c, 1).wait_recv()
            y_copy(c, 2).wait_recv()
            total = pair_sum(c, 0, 64) + r2[c, 0].astype(F32) + r2[c, 1].astype(F32)
            zst[c, 0:32] = total[32:64].astype(BF)
            z_copy(c).start()
            ownf[c, 0:32] = total[0:32]
        else:
            z_copy(c).wait_recv()
            put(c, ownf[c, 0:32] + r3[c, 0:32].astype(F32))

    def z_first(c, stage):
        forth, back = FORTH[TURN[c]], BACK[TURN[c]]
        if stage == 1:
            sib_copy(c).wait_recv()
            for i in range(4):
                zst[c, 32 * i : 32 * i + 32] = pair_sum(c, 64 * i + 32, 32).astype(BF)
            z_copy(c).start()
        elif stage == 2:
            z_copy(c).wait_recv()

            def total(at):
                return pair_sum(c, at, 32) + r3[c, at // 2 : at // 2 + 32].astype(F32)

            st[c, 128:160] = total(128).astype(BF)
            y_copy(c, 0).start()
            st[c, back : back + 32] = total(back).astype(BF)
            y_copy(c, 1).start()
            ownf[c, forth : forth + 32] = total(forth)
            ownf[c, 0:32] = total(0)
        elif stage == 3:
            y_copy(c, 0).wait_recv()
            st[c, forth : forth + 32] = (
                ownf[c, forth : forth + 32] + r1[c, 0:32].astype(F32)
            ).astype(BF)
            y_copy(c, 2).start()
        else:
            y_copy(c, 1).wait_recv()
            y_copy(c, 2).wait_recv()
            put(c, ownf[c, 0:32] + r2[c, 0, 0:32].astype(F32) + r2[c, 1, 0:32].astype(F32))

    def at_point(t):
        for c, stage in PLAN.get(t, ()):
            if c in ZFIRST:
                z_first(c, stage)
            else:
                y_first(c, stage)
        if t == 0:
            for item in far[1]:
                hx_copy(*item).start()
        if t == 3:
            pass_on(1)
        if t == 6:
            pass_on(0)
        if t == 9:
            pass_on(2)

    for c in range(NH):
        part = jnp.dot(g[...], wv[:, c * HC : (c + 1) * HC], preferred_element_type=F32)
        sibs[c] = part[256:512].astype(BF)
        sib_copy(c).start()
        ownf[c] = part[0:256]
        at_point(c)

    token256 = lax.broadcasted_iota(jnp.int32, (L, WC), 0).astype(F32).astype(BF)

    for dz in range(2):
        base = ((zl + dz) % 2) * 4
        if dz == 0:
            fw_copy(0).wait_recv()
        else:
            fw_copy(1).wait_recv()
            fw_copy(2).wait_recv()
        for n in range(NW):
            cols = slice(n * WC, (n + 1) * WC)
            for i in range(4):
                for s in range(2):
                    spot = pm[base + i, s : s + 1, cols].astype(BF)
                    val = ds[s, pl.ds(base + i, 1), cols].astype(BF)
                    r = (i * 2 + s) * L
                    gc[r : r + L, :] = jnp.where(token256 == spot, val, jnp.zeros((), BF))
            out = lax.dot_general(
                gc[...],
                hx[pl.ds(base, 4)].reshape(4 * 2 * L, DB),
                (((0,), (0,)), ((), ())),
                preferred_element_type=F32,
            )
            rows = slice(n * WC, min((n + 1) * WC, V))
            out = out[0 : rows.stop - rows.start]
            if dz == 0:
                gw_out[rows, :] = out
            else:
                gw_out[rows, :] += out
            at_point(NH + dz * NW + n)

    for t in range(NH + 2 * NW, NH + 2 * NW + 4):
        at_point(t)

    all_of(pm.at[0:7], pm_s, pm_r).wait_send()
    all_of(sel.at[0:7], sel_s, sel_r).wait_send()
    all_of(dl.at[1:NJ], dl_s, dl_r).wait_send()
    all_of(hx.at[0:3, 0], hx_s.at[0], hx_r.at[0, 0, 0]).wait_send()
    for sub in range(2):
        all_of(hx.at[0:2, 0], hx_s.at[1 + sub], hx_r.at[0, 0, 0]).wait_send()
    for which in range(3):
        fw_copy(which).wait_send()
    for c in range(NH):
        all_of(st.at[c, 0 : 3 * height(c)], y_s.at[c], y_r.at[c, 0]).wait_send()
        z_copy(c).wait_send()
    all_of(sibs, sib_s, sib_r.at[0]).wait_send()


def local(hidden, weight, bias, positions, lengths, pairs, margins):
    vmem = pl.BlockSpec(memory_space=pltpu.VMEM)
    smem = pl.BlockSpec(memory_space=pltpu.SMEM)
    hbm = pl.BlockSpec(memory_space=pl.ANY)
    dma = pltpu.SemaphoreType.DMA
    scratch = [
        pltpu.VMEM((VP, D), BF),
        pltpu.VMEM((2, 2, 2, L // 4, D), BF),
        pltpu.VMEM((NK, 2, 2, 2, L // 4, DB), BF),
        pltpu.VMEM((2 * L, VP), BF),
        pltpu.VMEM((NK * L, WC), BF),
        pltpu.VMEM((NH, 256, HC), BF),
        pltpu.VMEM((NH, 256, HC), BF),
        pltpu.VMEM((NH, 256, HC), F32),
        pltpu.VMEM((NH, 256, HC), BF),
        pltpu.VMEM((NH, 64, HC), BF),
        pltpu.VMEM((NH, 2, 64, HC), BF),
        pltpu.VMEM((NH, 128, HC), BF),
        pltpu.VMEM((NH, 128, HC), BF),
        pltpu.VMEM((NK, 4, VP), F32),
        pltpu.VMEM((NK, 2, VP), F32),
        pltpu.VMEM((NJ, NK, 128), F32),
        pltpu.VMEM((NK, VP), F32),
        pltpu.VMEM((NK, VP), F32),
        pltpu.VMEM((2, NK, VP), F32),
        dma((NF + 1,)),
        dma((2,)),
        dma,
        dma,
        dma,
        dma((3,)),
        dma((7, 2, 2)),
        dma((3,)),
        dma((3,)),
        dma,
        dma,
        dma,
        dma,
        dma,
        dma((NH,)),
        dma((NH,)),
        dma((NH, 3)),
        dma((NH,)),
        dma((NH,)),
    ]
    gh, gw = pl.pallas_call(
        kernel,
        out_shape=(
            pltpu.VMEM((2, 16, D), BF),
            pltpu.VMEM((V, DB), F32),
        ),
        in_specs=[hbm, hbm, vmem, vmem, smem, smem, smem],
        out_specs=(vmem, vmem),
        scratch_shapes=scratch,
        compiler_params=pltpu.CompilerParams(
            collective_id=0, has_side_effects=True, vmem_limit_bytes=56 * 2**20
        ),
        cost_estimate=pl.CostEstimate(
            flops=6 * 512 * V * D, bytes_accessed=24 * 2**20, transcendentals=0
        ),
        name="splade_backward",
    )(
        hidden.reshape(2, 2, 2, L // 4, D),
        weight,
        bias.reshape(1, V),
        positions,
        lengths.reshape(2),
        pairs.reshape(2),
        margins,
    )
    return gh.reshape(2, 1, 16, D), gw


def solution(mesh):
    in_specs = (
        P(None, "dp", None, None),
        P("vocab", None),
        P("vocab"),
        P(None, "dp", "vocab"),
        P(None, "dp"),
        P("dp", None),
        P("dp"),
    )
    out_specs = (P(None, "dp", "vocab", None), P("vocab", "dp"))
    return jax.shard_map(local, mesh=mesh, in_specs=in_specs, out_specs=out_specs, check_vma=False)
```

```python
import jax
import jax.numpy as jnp
from jax import lax
from jax.experimental import pallas as pl
from jax.experimental.pallas import tpu as pltpu
from jax.sharding import PartitionSpec as P

logit_divisor = 16.0
objective_factor = 256.0
regularizer_coefficient = 0.1

BF = jnp.bfloat16
F32 = jnp.float32
MESH = pl.DeviceIdType.MESH

V = 2000
VP = 2048
D = 4096
L = 256
NK = 8
NJ = 16
DB = 512
FWD = ((0, 256), (256, 256), (512, 512), (1024, 1024))
NF = len(FWD)
HC = 512
NH = D // HC
WC = 512
NW = VP // WC
ZFIRST = (0, 4, 7)
TURN = (0, 1, 0, 1, 1, 1, 0, 0)
FORTH, BACK = (64, 192), (192, 64)
PLAN = {
    2: ((0, 1),),
    3: ((1, 1),),
    4: ((2, 1),),
    5: ((3, 1),),
    6: ((1, 2), (4, 1), (5, 1)),
    7: ((0, 2), (2, 2)),
    8: ((3, 2), (1, 3), (6, 1), (7, 1)),
    9: ((0, 3), (5, 2)),
    10: ((2, 3), (4, 2), (3, 3), (1, 4)),
    11: ((0, 4), (6, 2)),
    12: ((5, 3), (7, 2)),
    13: ((2, 4), (3, 4), (4, 3)),
    14: ((6, 3), (7, 3)),
    15: ((4, 4), (5, 4), (7, 4), (6, 4)),
}


def kernel(
    h_hbm,
    w_hbm,
    bias,
    pos_in,
    lens,
    pairs,
    margins,
    gh_out,
    gw_out,
    wv,
    hv,
    hx,
    g,
    gc,
    sibs,
    sibr,
    ownf,
    st,
    r1,
    r2,
    zst,
    r3,
    pm,
    sel,
    dl,
    qs,
    ps,
    ds,
    w_sem,
    h_sem,
    own_sem,
    pm_s,
    pm_r,
    hx_s,
    hx_r,
    fw_s,
    fw_r,
    sel_s,
    sel_r,
    dl_s,
    dl_r,
    sib_s,
    sib_r,
    y_s,
    y_r,
    z_s,
    z_r,
):
    k = lax.axis_index("dp")
    j = lax.axis_index("vocab")
    core = j % 2
    y = (j // 2) % 4
    zh = j // 8
    zl = k // 4
    x = k % 4

    def vid(zrel, yrel, crel):
        return ((zh + zrel) % 2) * 8 + ((y + yrel) % 4) * 2 + (core + crel) % 2

    def kid(dz, dx):
        return ((zl + dz) % 2) * 4 + (x + dx) % 4

    sibling = vid(0, 0, 1)
    up = vid(0, 1, 0)
    down = vid(0, 3, 0)
    across = vid(1, 0, 0)
    dp_steps = [(dz, dx) for dz in range(2) for dx in range(4) if (dz, dx) != (0, 0)]

    halves = (slice(0, D // 2), slice(D // 2, D))
    h_copies = [
        pltpu.make_async_copy(h_hbm.at[..., cols], hv.at[..., cols], h_sem.at[i])
        for i, cols in enumerate(halves)
    ]
    w0_copies = [
        pltpu.make_async_copy(
            w_hbm.at[0 : FWD[0][1], cols], wv.at[0 : FWD[0][1], cols], w_sem.at[(0, NF)[i]]
        )
        for i, cols in enumerate(halves)
    ]
    w_copies = [None]
    for n, (at, size) in enumerate(FWD):
        if n > 0:
            rows = min(size, V - at)
            c = pltpu.make_async_copy(
                w_hbm.at[pl.ds(at, rows), :], wv.at[pl.ds(at, rows), :], w_sem.at[n]
            )
            w_copies.append(c)
    h_copies[0].start()
    w0_copies[0].start()

    barrier = pltpu.get_barrier_semaphore()
    for dz, dx in dp_steps:
        pl.semaphore_signal(barrier, inc=1, device_id={"dp": kid(dz, dx)}, device_id_type=MESH)
    for dx in range(1, 4):
        pl.semaphore_signal(
            barrier,
            inc=1,
            device_id={"dp": kid(1, dx), "vocab": across},
            device_id_type=MESH,
        )
    for i in range(1, NJ):
        zr, yr, cr = i // 8, (i // 2) % 4, i % 2
        pl.semaphore_signal(
            barrier,
            inc=1,
            device_id={"dp": kid(zr, 0), "vocab": vid(zr, yr, cr)},
            device_id_type=MESH,
        )
    pl.semaphore_signal(barrier, inc=1, device_id={"vocab": across}, device_id_type=MESH)

    h_copies[1].start()
    w0_copies[1].start()
    own_copy = pltpu.make_async_copy(
        hv.at[core, :, :, :, pl.ds(pl.multiple_of(k * DB, DB), DB)],
        hx.at[k, core],
        own_sem,
    )
    wv[V:VP, :] = jnp.zeros((VP - V, D), BF)

    pad = jnp.zeros((1, VP - V), F32)
    for s in range(2):
        pm[k, s : s + 1, :] = jnp.concatenate([pos_in[s].astype(F32), pad], axis=1)
    pm[k, 2:3, 0:128] = jnp.full((1, 128), pairs[0], jnp.int32).astype(F32)
    pm[k, 2:3, 128:256] = jnp.full((1, 128), pairs[1], jnp.int32).astype(F32)
    pm[k, 2:3, 256:384] = jnp.full((1, 128), margins[0], F32)
    pm[k, 2:3, 384:VP] = jnp.zeros((1, VP - 384), F32)
    pm[k, 3:4, :] = jnp.zeros((1, VP), F32)

    def all_of(ref, ssem, rsem):
        return pltpu.make_async_remote_copy(
            src_ref=ref,
            dst_ref=ref,
            send_sem=ssem,
            recv_sem=rsem,
            device_id={"vocab": sibling},
            device_id_type=MESH,
        )

    def to_dp(ref, ssem, rsem, i):
        dz, dx = dp_steps[i]
        return pltpu.make_async_remote_copy(
            src_ref=ref.at[k],
            dst_ref=ref.at[k],
            send_sem=ssem,
            recv_sem=rsem,
            device_id={"dp": kid(dz, dx)},
            device_id_type=MESH,
        )

    near = [(i, None, None) for i in range(7) if dp_steps[i][0] == 0]
    far = [
        [(i, part, sub) for i in range(7) if dp_steps[i][0] == 1 for part in range(2)]
        for sub in range(2)
    ]

    def hx_copy(i, part, sub):
        dz, dx = dp_steps[i]
        other = kid(dz, dx)
        cols = pl.ds(pl.multiple_of(other * DB, DB), DB)
        if part is None:
            src, dst = hv.at[core, :, :, :, cols], hx.at[k, core]
            to = {"dp": other}
        else:
            src, dst = hv.at[core, part, sub, :, cols], hx.at[k, core, part, sub]
            to = {"dp": other, "vocab": vid(part, 0, 0)}
        return pltpu.make_async_remote_copy(
            src_ref=src,
            dst_ref=dst,
            send_sem=hx_s.at[0 if part is None else 1 + sub],
            recv_sem=hx_r.at[0 if part is None else 1 + sub],
            device_id=to,
            device_id_type=MESH,
        )

    def fw_copy(which):
        if which == 0:
            ref = hx.at[pl.ds(zl * 4, 4), core]
        else:
            ref = hx.at[pl.ds((1 - zl) * 4, 4), core, :, which - 1]
        return pltpu.make_async_remote_copy(
            src_ref=ref,
            dst_ref=ref,
            send_sem=fw_s.at[which],
            recv_sem=fw_r.at[which],
            device_id={"vocab": sibling},
            device_id_type=MESH,
        )

    def pass_on(which):
        if which == 0:
            own_copy.wait()
        all_of(hx.at[0 : 3 if which == 0 else 2, 0], hx_s.at[which], hx_r.at[which]).wait_recv()
        fw_copy(which).start()

    def logits(rows, cols):
        return lax.dot_general(
            hv[..., cols].reshape(2 * L, cols.stop - cols.start),
            wv[rows, cols],
            (((1,), (1,)), ((), ())),
            preferred_element_type=F32,
        )

    pl.semaphore_wait(barrier, len(dp_steps) + 3 + NJ)
    for i in range(7):
        to_dp(pm, pm_s, pm_r, i).start()
    for n, (at, size) in enumerate(FWD):
        rows = slice(at, at + size)
        if n == 0:
            h_copies[0].wait()
            w0_copies[0].wait()
            w_copies[1].start()
            lg = logits(rows, halves[0])
            h_copies[1].wait()
            w0_copies[1].wait()
            for item in far[0]:
                hx_copy(*item).start()
            own_copy.start()
            w_copies[2].start()
            lg += logits(rows, halves[1])
        else:
            w_copies[n].wait()
            if 2 < n + 2 < NF:
                w_copies[n + 2].start()
            lg = logits(rows, slice(0, D))
        token = lax.broadcasted_iota(jnp.int32, (L, size), 0).astype(F32)
        width = min(size, V - at)
        for s in range(2):
            spot = pm[k, s : s + 1, at : at + size]
            picked = jnp.sum(
                jnp.where(token == spot, lg[s * L : (s + 1) * L], 0.0), axis=0, keepdims=True
            )
            b = bias[:, at : at + width]
            if width < size:
                b = jnp.concatenate([b, jnp.zeros((1, size - width), F32)], axis=1)
            valid = spot < lens[s].astype(F32)
            sel[k, s : s + 1, at : at + size] = jnp.where(valid, jnp.maximum(picked + b, 0.0), 0.0)

    for i in range(7):
        to_dp(sel, sel_s, sel_r, i).start()
    all_of(pm.at[0:7], pm_s, pm_r).wait_recv()
    first = jnp.concatenate([pm[i, 2:3, 0:128] for i in range(NK)], axis=0)
    second = jnp.concatenate([pm[i, 2:3, 128:256] for i in range(NK)], axis=0)
    margin = jnp.concatenate([pm[i, 2:3, 256:384] for i in range(NK)], axis=0)

    all_of(sel.at[0:7], sel_s, sel_r).wait_recv()
    for i in range(NK):
        qs[i : i + 1, :] = sel[i, 0:1, :]
        ps[i : i + 1, :] = sel[i, 1:2, :]
    q = jnp.log1p(qs[...])
    p = jnp.log1p(ps[...])
    def hit(a, b):
        return jnp.where(a == b, 1.0, 0.0)

    diff = jnp.zeros((NK, VP), F32)
    for i in range(NK):
        sign = hit(first, float(i)) - hit(second, float(i))
        diff += jnp.tile(sign, (1, VP // 128)) * p[i : i + 1, :]
    dl[j] = jnp.broadcast_to(jnp.sum(q * diff, axis=1, keepdims=True), (NK, 128))

    def dl_copy(i):
        zr, yr, cr = i // 8, (i // 2) % 4, i % 2
        return pltpu.make_async_remote_copy(
            src_ref=dl.at[j],
            dst_ref=dl.at[j],
            send_sem=dl_s,
            recv_sem=dl_r,
            device_id={"dp": kid(zr, 0), "vocab": vid(zr, yr, cr)},
            device_id_type=MESH,
        )

    for i in range(1, NJ):
        dl_copy(i).start()
    for item in near:
        hx_copy(*item).start()

    reg = objective_factor * regularizer_coefficient * 2.0 / NK / NK
    mean_q = reg * jnp.sum(q, axis=0, keepdims=True)
    mean_p = reg * jnp.sum(p, axis=0, keepdims=True)
    inv_q = jnp.where(qs[...] > 0.0, 1.0 / (1.0 + qs[...]), 0.0)
    inv_p = jnp.where(ps[...] > 0.0, 1.0 / (1.0 + ps[...]), 0.0)

    all_of(dl.at[1:NJ], dl_s, dl_r).wait_recv()
    delta = dl[0]
    for i in range(1, NJ):
        delta += dl[i]
    delta = delta / logit_divisor
    weight_of = (objective_factor * 2.0 / NK / logit_divisor) * (delta - margin)
    ds[0] = (jnp.tile(weight_of, (1, VP // 128)) * diff + mean_q) * inv_q
    row = lax.broadcasted_iota(jnp.int32, (NK, 128), 0).astype(F32)
    dp = jnp.zeros((NK, VP), F32)
    for i in range(NK):
        sign = hit(first[i : i + 1, :], row) - hit(second[i : i + 1, :], row)
        dp += jnp.tile(sign * weight_of[i : i + 1, :], (1, VP // 128)) * q[i : i + 1, :]
    ds[1] = (dp + mean_p) * inv_p

    token16 = lax.broadcasted_iota(jnp.int32, (16, VP), 0).astype(F32)
    own_d = [ds[s, pl.ds(k, 1), :].astype(BF) for s in range(2)]
    own_p = [pm[k, s : s + 1, :].astype(BF) for s in range(2)]
    for crel in range(2):
        for yrel in range(4):
            for zrel in range(2):
                base = (vid(zrel, yrel, crel) * 16).astype(F32)
                token = (token16 + base).astype(BF)
                for s in range(2):
                    r = crel * 256 + yrel * 64 + zrel * 32 + s * 16
                    g[r : r + 16, :] = jnp.where(token == own_p[s], own_d[s], jnp.zeros((), BF))

    def height(c):
        return 32 if c in ZFIRST else 64

    def sib_copy(c):
        return pltpu.make_async_remote_copy(
            src_ref=sibs.at[c],
            dst_ref=sibr.at[c],
            send_sem=sib_s,
            recv_sem=sib_r.at[c],
            device_id={"vocab": sibling},
            device_id_type=MESH,
        )

    def y_copy(c, which):
        n = height(c)
        side = TURN[c]
        src = st.at[c, pl.ds((128, BACK[side], FORTH[side])[which], n)]
        if which == 0:
            dst = r1.at[c, 0:n]
        else:
            dst = r2.at[c, which - 1, 0:n]
        return pltpu.make_async_remote_copy(
            src_ref=src,
            dst_ref=dst,
            send_sem=y_s.at[c],
            recv_sem=y_r.at[c, min(which, 1)],
            device_id={"vocab": (up, down)[side if which != 1 else 1 - side]},
            device_id_type=MESH,
        )

    def z_copy(c):
        n = 128 if c in ZFIRST else 32
        return pltpu.make_async_remote_copy(
            src_ref=zst.at[c, 0:n],
            dst_ref=r3.at[c, 0:n],
            send_sem=z_s.at[c],
            recv_sem=z_r.at[c],
            device_id={"vocab": across},
            device_id_type=MESH,
        )

    def pair_sum(c, at, n):
        return ownf[c, at : at + n] + sibr[c, at : at + n].astype(F32)

    def put(c, total):
        gh_out[0, :, c * HC : (c + 1) * HC] = total[0:16].astype(BF)
        gh_out[1, :, c * HC : (c + 1) * HC] = total[16:32].astype(BF)

    def y_first(c, stage):
        forth, back = FORTH[TURN[c]], BACK[TURN[c]]
        if stage == 1:
            sib_copy(c).wait_recv()
            st[c, 128:192] = pair_sum(c, 128, 64).astype(BF)
            y_copy(c, 0).start()
            st[c, back : back + 64] = pair_sum(c, back, 64).astype(BF)
            y_copy(c, 1).start()
        elif stage == 2:
            y_copy(c, 0).wait_recv()
            st[c, forth : forth + 64] = (pair_sum(c, forth, 64) + r1[c].astype(F32)).astype(BF)
            y_copy(c, 2).start()
        elif stage == 3:
            all_of(r2.at[c, :, 0 : height(c)], y_s.at[c], y_r.at[c, 1]).wait_recv()
            total = pair_sum(c, 0, 64) + r2[c, 0].astype(F32) + r2[c, 1].astype(F32)
            zst[c, 0:32] = total[32:64].astype(BF)
            z_copy(c).start()
            ownf[c, 0:32] = total[0:32]
        else:
            z_copy(c).wait_recv()
            put(c, ownf[c, 0:32] + r3[c, 0:32].astype(F32))

    def z_first(c, stage):
        forth, back = FORTH[TURN[c]], BACK[TURN[c]]
        if stage == 1:
            sib_copy(c).wait_recv()
            for i in range(4):
                zst[c, 32 * i : 32 * i + 32] = pair_sum(c, 64 * i + 32, 32).astype(BF)
            z_copy(c).start()
        elif stage == 2:
            z_copy(c).wait_recv()

            def total(at):
                return pair_sum(c, at, 32) + r3[c, at // 2 : at // 2 + 32].astype(F32)

            st[c, 128:160] = total(128).astype(BF)
            y_copy(c, 0).start()
            st[c, back : back + 32] = total(back).astype(BF)
            y_copy(c, 1).start()
            ownf[c, forth : forth + 32] = total(forth)
            ownf[c, 0:32] = total(0)
        elif stage == 3:
            y_copy(c, 0).wait_recv()
            st[c, forth : forth + 32] = (
                ownf[c, forth : forth + 32] + r1[c, 0:32].astype(F32)
            ).astype(BF)
            y_copy(c, 2).start()
        else:
            all_of(r2.at[c, :, 0 : height(c)], y_s.at[c], y_r.at[c, 1]).wait_recv()
            put(c, ownf[c, 0:32] + r2[c, 0, 0:32].astype(F32) + r2[c, 1, 0:32].astype(F32))

    def at_point(t):
        for c, stage in PLAN.get(t, ()):
            if c in ZFIRST:
                z_first(c, stage)
            else:
                y_first(c, stage)
        if t == 0:
            for item in far[1]:
                hx_copy(*item).start()
        if t == 3:
            pass_on(1)
        if t == 6:
            pass_on(0)
        if t == 9:
            pass_on(2)

    for c in range(NH):
        part = jnp.dot(g[...], wv[:, c * HC : (c + 1) * HC], preferred_element_type=F32)
        sibs[c] = part[256:512].astype(BF)
        sib_copy(c).start()
        ownf[c] = part[0:256]
        at_point(c)

    token256 = lax.broadcasted_iota(jnp.int32, (L, WC), 0).astype(F32).astype(BF)

    for dz in range(2):
        base = ((zl + dz) % 2) * 4
        if dz == 0:
            fw_copy(0).wait_recv()
        else:
            fw_copy(1).wait_recv()
            fw_copy(2).wait_recv()
        for n in range(NW):
            cols = slice(n * WC, (n + 1) * WC)
            for i in range(4):
                for s in range(2):
                    spot = pm[base + i, s : s + 1, cols].astype(BF)
                    val = ds[s, pl.ds(base + i, 1), cols].astype(BF)
                    r = (i * 2 + s) * L
                    gc[r : r + L, :] = jnp.where(token256 == spot, val, jnp.zeros((), BF))
            out = lax.dot_general(
                gc[...],
                hx[pl.ds(base, 4)].reshape(4 * 2 * L, DB),
                (((0,), (0,)), ((), ())),
                preferred_element_type=F32,
            )
            rows = slice(n * WC, min((n + 1) * WC, V))
            out = out[0 : rows.stop - rows.start]
            if dz == 0:
                gw_out[rows, :] = out
            else:
                gw_out[rows, :] += out
            at_point(NH + dz * NW + n)

    for t in range(NH + 2 * NW, NH + 2 * NW + 4):
        at_point(t)

    all_of(pm.at[0:7], pm_s, pm_r).wait_send()
    all_of(sel.at[0:7], sel_s, sel_r).wait_send()
    all_of(dl.at[1:NJ], dl_s, dl_r).wait_send()
    all_of(hx.at[0:3, 0], hx_s.at[0], hx_r.at[0]).wait_send()
    for sub in range(2):
        all_of(hx.at[0:2, 0], hx_s.at[1 + sub], hx_r.at[0]).wait_send()
    for which in range(3):
        fw_copy(which).wait_send()
    for c in range(NH):
        all_of(st.at[c, 0 : 3 * height(c)], y_s.at[c], y_r.at[c, 0]).wait_send()
        z_copy(c).wait_send()
    all_of(sibs, sib_s, sib_r.at[0]).wait_send()


def local(hidden, weight, bias, positions, lengths, pairs, margins):
    vmem = pl.BlockSpec(memory_space=pltpu.VMEM)
    smem = pl.BlockSpec(memory_space=pltpu.SMEM)
    hbm = pl.BlockSpec(memory_space=pl.ANY)
    dma = pltpu.SemaphoreType.DMA
    scratch = [
        pltpu.VMEM((VP, D), BF),
        pltpu.VMEM((2, 2, 2, L // 4, D), BF),
        pltpu.VMEM((NK, 2, 2, 2, L // 4, DB), BF),
        pltpu.VMEM((2 * L, VP), BF),
        pltpu.VMEM((NK * L, WC), BF),
        pltpu.VMEM((NH, 256, HC), BF),
        pltpu.VMEM((NH, 256, HC), BF),
        pltpu.VMEM((NH, 256, HC), F32),
        pltpu.VMEM((NH, 256, HC), BF),
        pltpu.VMEM((NH, 64, HC), BF),
        pltpu.VMEM((NH, 2, 64, HC), BF),
        pltpu.VMEM((NH, 128, HC), BF),
        pltpu.VMEM((NH, 128, HC), BF),
        pltpu.VMEM((NK, 4, VP), F32),
        pltpu.VMEM((NK, 2, VP), F32),
        pltpu.VMEM((NJ, NK, 128), F32),
        pltpu.VMEM((NK, VP), F32),
        pltpu.VMEM((NK, VP), F32),
        pltpu.VMEM((2, NK, VP), F32),
        dma((NF + 1,)),
        dma((2,)),
        dma,
        dma,
        dma,
        dma((3,)),
        dma((3,)),
        dma((3,)),
        dma((3,)),
        dma,
        dma,
        dma,
        dma,
        dma,
        dma((NH,)),
        dma((NH,)),
        dma((NH, 2)),
        dma((NH,)),
        dma((NH,)),
    ]
    gh, gw = pl.pallas_call(
        kernel,
        out_shape=(
            pltpu.VMEM((2, 16, D), BF),
            pltpu.VMEM((V, DB), F32),
        ),
        in_specs=[hbm, hbm, vmem, vmem, smem, smem, smem],
        out_specs=(vmem, vmem),
        scratch_shapes=scratch,
        compiler_params=pltpu.CompilerParams(
            collective_id=0, has_side_effects=True, vmem_limit_bytes=56 * 2**20
        ),
        cost_estimate=pl.CostEstimate(
            flops=6 * 512 * V * D, bytes_accessed=24 * 2**20, transcendentals=0
        ),
        name="splade_backward",
    )(
        hidden.reshape(2, 2, 2, L // 4, D),
        weight,
        bias.reshape(1, V),
        positions,
        lengths.reshape(2),
        pairs.reshape(2),
        margins,
    )
    return gh.reshape(2, 1, 16, D), gw


def solution(mesh):
    in_specs = (
        P(None, "dp", None, None),
        P("vocab", None),
        P("vocab"),
        P(None, "dp", "vocab"),
        P(None, "dp"),
        P("dp", None),
        P("dp"),
    )
    out_specs = (P(None, "dp", "vocab", None), P("vocab", "dp"))
    return jax.shard_map(local, mesh=mesh, in_specs=in_specs, out_specs=out_specs, check_vma=False)
```
